512 devices in a mesh: dp: 64 (over x, z), tp: 8 (over y, core).
Axes of the slice: x: 4, y: 4, z: 16, core: 2. Of those that a mesh axis runs over, the one named last changes fastest.
Arguments:
- layer_input: bfloat16 [65536, 2560], P(('dp', 'tp')), may hold values from -6 to 6
- queries: bfloat16 [65536, 3072], P('dp', 'tp'), may hold values from -6 to 6
- key_vectors: bfloat16 [65536, 3072], P('dp', 'tp'), may hold values from -6 to 6
- out_grad: bfloat16 [65536, 3072], P('dp', 'tp'), may hold values from -6 to 6
- feedback: bfloat16 [163840, 3072], P('dp', 'tp'), may hold values from -48 to 48
- factor_prev: float32 [32, 3072], P(None, 'tp'), may hold values from -6 to 6
- token_count: int32 [64], P('dp'), may hold values from 204 to 1024, as said below
- segment_ids: int32 [65536], P('dp'), may hold values from 0 to 32, as said below
Outputs:
- basis: float32 [32, 2560], P(None, 'tp')
- factor_next: float32 [32, 3072], P(None, 'tp')
The draws below stay inside these ranges and needn't reach their ends.
Inputs may be any that keep to these rules, and one draw needn't show every extreme that they name: `token_count`: the number of real tokens of each replica's buffer of 1024 slots; later slots are padding; some replica is full. `segment_ids`: within each replica's 1024 slots the ids start at 0 and never fall, rising by at most one a slot; the first 16 slots of a replica share id 0; every replica holds exactly 33 documents.
All inputs are finite; a program needn't handle non-finite values.
Results may differ from the reference program's by a relative error of at most 0.0042.
Values may be sent and summed in bfloat16 or wider, within the bound.
A program may use at most 64 MiB of HBM per device.

```python
import math
import jax
import jax.numpy as jnp
from jax import lax

DW = 2560
HEAD_DIM = 128
RANK = 32
SLOTS = 1024
HEADS = 24
REPLICAS = 64


def draw_queries(key, part):
    key = jax.random.fold_in(key, 3)
    array_shape = (REPLICAS, SLOTS, HEADS * HEAD_DIM)
    drawn = jnp.clip(jax.random.normal(key, array_shape, jnp.float32), -6.0, 6.0)
    return drawn.reshape(REPLICAS * SLOTS, HEADS * HEAD_DIM).astype(jnp.bfloat16)


def draw_key_vectors(key, part):
    key = jax.random.fold_in(key, 5)
    array_shape = (REPLICAS, SLOTS, HEADS * HEAD_DIM)
    drawn = jnp.clip(jax.random.normal(key, array_shape, jnp.float32), -6.0, 6.0)
    return drawn.reshape(REPLICAS * SLOTS, HEADS * HEAD_DIM).astype(jnp.bfloat16)


def draw_token_count(key, part):
    key = jax.random.fold_in(key, 7)
    lower_key, pick_key = jax.random.split(key)
    floor_count = max(SLOTS // 5, 16)
    upper_count = max(SLOTS // 2, floor_count + SLOTS // 4)
    drawn = jax.random.randint(lower_key, (REPLICAS,), floor_count, upper_count + 1)
    fullest = jax.random.randint(pick_key, (), 0, REPLICAS)
    return jnp.where(jnp.arange(REPLICAS) == fullest, SLOTS, drawn).astype(jnp.int32)


def draw_segment_ids(key, part):
    key = jax.random.fold_in(key, 11)
    replica_keys = jax.random.split(key, REPLICAS)
    orders = jax.vmap(lambda single: jax.random.permutation(single, SLOTS - 16))(replica_keys)
    chosen = orders[:, :SLOTS // 32] + 16
    rows_index = jnp.broadcast_to(jnp.arange(REPLICAS)[:, None], chosen.shape)
    opening = jnp.zeros((REPLICAS, SLOTS), jnp.int32).at[rows_index, chosen].set(1)
    return jnp.cumsum(opening, axis=1).astype(jnp.int32).reshape(REPLICAS * SLOTS)


def block_scale(stream_key, shape, shards, low, high):
    gain = 1.0
    for dim, parts in shards:
        draws = jax.random.uniform(jax.random.fold_in(jax.random.fold_in(stream_key, 6), dim), (parts,), jnp.float32, low / len(shards), high / len(shards))
        gain = gain * jnp.repeat(jnp.exp(draws), shape[dim] // parts).reshape((-1,) + (1,) * (len(shape) - 1 - dim))
    return gain


def scatter_about(key, extent, width, limit, pieces=(), kind=jnp.bfloat16):
    values = jax.random.normal(key, extent, jnp.float32) * width
    if len(pieces) > 0:
        values = block_scale(key, extent, pieces, -0.22, 0.18) * values
    return jnp.clip(values, min=-limit, max=limit).astype(kind)


def setup_inputs(seed: int = 0) -> dict:
    key_of = jax.random.split(jax.random.key(seed), 9)
    return {
        "layer_input": scatter_about(key_of[0], (REPLICAS * SLOTS, DW), 1.0, 6.0, ((0, 512),)),
        "queries": draw_queries(jax.random.fold_in(key_of[8], 71), 0),
        "key_vectors": draw_key_vectors(jax.random.fold_in(key_of[8], 71), 0),
        "out_grad": scatter_about(key_of[3], (REPLICAS * SLOTS, HEADS * HEAD_DIM), 1.0, 6.0, ((0, 64), (1, 8))),
        "feedback": scatter_about(key_of[4], (REPLICAS * DW, HEADS * HEAD_DIM), 8.0, 48.0, ((0, 64), (1, 8))),
        "factor_prev": scatter_about(key_of[5], (RANK, HEADS * HEAD_DIM), 1.0, 6.0, ((1, 8),), jnp.float32),
        "token_count": draw_token_count(jax.random.fold_in(key_of[8], 71), 0),
        "segment_ids": draw_segment_ids(jax.random.fold_in(key_of[8], 71), 0),
    }


masked_score = -1e+30

def replica_values(query_rows, key_rows, grad_rows, live_count, segments):
    length = query_rows.shape[0]
    head_count = query_rows.shape[1] // HEAD_DIM
    query_heads = query_rows.astype(jnp.float32).reshape(length, head_count, HEAD_DIM)
    key_heads = key_rows.astype(jnp.float32).reshape(length, head_count, HEAD_DIM)
    grad_heads = grad_rows.astype(jnp.float32).reshape(length, head_count, HEAD_DIM)
    positions = jnp.arange(length, dtype=jnp.int32)
    block_size = min(512, length)
    summed = jnp.zeros((length, head_count, HEAD_DIM), jnp.float32)
    for number in range(length // block_size):
        first_row = number * block_size
        last_row = first_row + block_size
        scores = jnp.einsum('qhd,khd->hqk', query_heads[first_row:last_row], key_heads[:last_row], precision=lax.Precision.HIGHEST) * HEAD_DIM ** (-0.5)
        query_pos = positions[first_row:last_row]
        key_pos = positions[:last_row]
        allowed = (segments[first_row:last_row, None] == segments[None, :last_row]) & (key_pos[None, :] <= query_pos[:, None]) & (query_pos[:, None] < live_count) & (key_pos[None, :] < live_count)
        masked = jnp.where(allowed[None], scores, masked_score)
        highest = lax.optimization_barrier(jnp.max(masked, axis=-1, keepdims=True))
        raised = jnp.where(allowed[None], jnp.exp(masked - highest), 0.0)
        totals = jnp.maximum(lax.optimization_barrier(jnp.sum(raised, axis=-1, keepdims=True)), 1.0)
        weights = (raised / totals).astype(jnp.bfloat16)
        summed = summed.at[:last_row].add(jnp.einsum('hqk,qhd->khd', weights.astype(jnp.float32), grad_heads[first_row:last_row], precision=lax.Precision.HIGHEST))
    return summed.reshape(length, -1).astype(jnp.bfloat16)

def reference(layer_input, queries, key_vectors, out_grad, feedback, factor_prev, token_count, segment_ids):
    precise = lax.Precision.HIGHEST
    features = queries.shape[1]
    inputs_all = layer_input.reshape(REPLICAS, SLOTS, DW)
    queries_all = queries.reshape(REPLICAS, SLOTS, features)
    keys_all = key_vectors.reshape(REPLICAS, SLOTS, features)
    grads_all = out_grad.reshape(REPLICAS, SLOTS, features)
    feedback_all = feedback.reshape(REPLICAS, DW, features)
    segments_all = segment_ids.reshape(REPLICAS, SLOTS)

    def first_pass(running, sliced):
        inputs, query_rows, key_rows, grad_rows, carried, live_count, segments = sliced
        values = replica_values(query_rows, key_rows, grad_rows, live_count, segments)
        matrix = jnp.dot(inputs.T.astype(jnp.float32), values.astype(jnp.float32), preferred_element_type=jnp.float32) + carried.astype(jnp.float32)
        return (running + lax.dot_general(factor_prev, matrix, (((1,), (1,)), ((), ())), precision=precise), values)
    left_factor, values_all = lax.scan(first_pass, jnp.zeros((factor_prev.shape[0], DW), jnp.float32), (inputs_all, queries_all, keys_all, grads_all, feedback_all, token_count, segments_all))
    gram_matrix = jnp.dot(left_factor, left_factor.T, precision=precise)
    cholesky_low = jnp.linalg.cholesky(gram_matrix)
    orthonormal = lax.linalg.triangular_solve(cholesky_low, left_factor, left_side=True, lower=True)

    def second_pass(running, sliced):
        inputs, values, carried = sliced
        matrix = jnp.dot(inputs.T.astype(jnp.float32), values.astype(jnp.float32), preferred_element_type=jnp.float32) + carried.astype(jnp.float32)
        return (running + jnp.dot(orthonormal, matrix, precision=precise), None)
    right_factor, unused = lax.scan(second_pass, jnp.zeros((factor_prev.shape[0], features), jnp.float32), (inputs_all, values_all, feedback_all))
    return (orthonormal * math.sqrt(DW), right_factor / REPLICAS)
```

```python
import math

import jax
import jax.numpy as jnp
from jax import lax
from jax.experimental import pallas as pl
from jax.experimental.pallas import tpu as pltpu
from jax.sharding import PartitionSpec as P

MESH = pl.DeviceIdType.MESH
F32, BF16 = jnp.float32, jnp.bfloat16
NT = (((1,), (1,)), ((), ()))

NX, NY, NZ, NC = 4, 4, 16, 2
GROUP = NY * NC
PLANE = NX * GROUP

HEAD_DIM = 128
HEADS = 3
SLOTS = 1024
WIDTH = 2560
RANK = 32
LANES = 128
HALF = 16
FEATURES = HEADS * HEAD_DIM
TILES = WIDTH // LANES
MAIN = NX * NY
BLOCK = 256
BLOCKS = SLOTS // BLOCK
MASKED = -1e30


def hops(step, size):
    return min(step, size - step)


PLANE_STEPS = sorted(
    [
        (dx, dy, dc)
        for dx in range(NX)
        for dy in range(NY)
        for dc in range(NC)
        if (dx, dy, dc) != (0, 0, 0)
    ],
    key=lambda s: -(hops(s[0], NX) * 2 + hops(s[1], NY) * 2 + s[2]),
)
GROUP_STEPS = [s for s in PLANE_STEPS if s[0] == 0]
ROW_STEPS = sorted(range(1, NX), key=lambda s: -hops(s, NX))
DEPTH_STEPS = sorted(range(1, NZ), key=lambda s: -hops(s, NZ))
HOLDERS = [(xh, (xh + 2 * ch) % NY, ch) for ch in range(NC) for xh in range(NX)]


def segment_starts(seg, count):
    rows = lax.broadcasted_iota(jnp.int32, seg.shape, 0)
    lanes = lax.broadcasted_iota(jnp.int32, seg.shape, 1)
    slot = rows * LANES + lanes
    wrapped = pltpu.roll(seg, 1, 1)
    before = jnp.where(lanes == 0, pltpu.roll(wrapped, 1, 0), wrapped)
    first = jnp.where((seg != before) & (slot > 0), slot, 0)
    step = 1
    while step < LANES:
        first = jnp.maximum(first, jnp.where(lanes >= step, pltpu.roll(first, step, 1), 0))
        step *= 2
    carry = jnp.broadcast_to(jnp.max(first, axis=1, keepdims=True), first.shape)
    step = 1
    while step < SLOTS // LANES:
        carry = jnp.maximum(carry, jnp.where(rows >= step, pltpu.roll(carry, step, 0), 0))
        step *= 2
    first = jnp.maximum(first, jnp.where(rows >= 1, pltpu.roll(carry, 1, 0), 0))
    return jnp.where(slot < count, first, 4 * SLOTS)


def split(value):
    high = value.astype(BF16)
    low = (value - high.astype(F32)).astype(BF16)
    return jnp.concatenate([high, low], axis=0)


def attend(head, starts, k_ref, q_ref, g_ref, w_ref, v_ref):
    lanes = slice(head * HEAD_DIM, (head + 1) * HEAD_DIM)
    rate = HEAD_DIM ** (-0.5) * math.log2(math.e)
    for b in range(BLOCKS):
        low, high = b * BLOCK, (b + 1) * BLOCK
        q = q_ref[low:high, lanes]
        start = starts[b]
        live = start < SLOTS
        key = lax.broadcasted_iota(jnp.int32, (BLOCK, BLOCK), 0) + low
        query = lax.broadcasted_iota(jnp.int32, (BLOCK, BLOCK), 1) + low
        near = lax.dot_general(k_ref[low:high, lanes], q, NT, preferred_element_type=F32)
        near = jnp.where((key >= start) & (key <= query), near, MASKED)
        top = jnp.max(near, axis=0, keepdims=True)
        if b:
            far = lax.dot_general(k_ref[0:low, lanes], q, NT, preferred_element_type=F32)
            far_key = lax.broadcasted_iota(jnp.int32, (low, BLOCK), 0)
            far = jnp.where(far_key >= start, far, MASKED)
            top = jnp.maximum(top, jnp.max(far, axis=0, keepdims=True))
        near = jnp.exp2((near - top) * rate)
        total = jnp.sum(near, axis=0, keepdims=True)
        if b:
            far = jnp.exp2((far - top) * rate)
            total = total + jnp.sum(far, axis=0, keepdims=True)
        scale = jnp.where(live, 1.0 / jnp.maximum(total, 1.0), 0.0)
        w_ref[low:high, low:high] = (near * scale).astype(BF16)
        if b:
            w_ref[0:low, low:high] = (far * scale).astype(BF16)
    for b in range(BLOCKS):
        low, high = b * BLOCK, (b + 1) * BLOCK
        v = jnp.dot(w_ref[low:high, low:], g_ref[low:, lanes], preferred_element_type=F32)
        v_ref[low:high, lanes] = v.astype(BF16)


def kernel(
    layer_ref, q_hbm, k_hbm, g_hbm, feedback_ref, factor_ref, count_ref, segment_ref,
    basis_ref, next_ref,
    q_ref, k_ref, g_ref, f_ref, l_ref, v_ref, w_ref, pf_ref,
    zs_ref, zr_ref, part_ref, main_ref, extra_ref, deep_ref, left_ref, t_ref, ys_ref, xr_ref, deep2_ref, yf_ref,
    load_sem,
    a_send, a_recv, rs_send, rs_main, rs_extra, d_send, d_recv, ag_send, ag_main, ag_extra,
    t_send, t_recv, x_send, x_recv, d2_send, d2_recv, xg_send, xg_recv,
):
    dp, tp = lax.axis_index("dp"), lax.axis_index("tp")
    x, z = dp // NZ, dp % NZ
    y, c = tp // NC, tp % NC
    place = x * GROUP + tp

    def plane_peer(step):
        dx, dy, dc = step
        px, py, pc = (x + dx) % NX, (y + dy) % NY, (c + dc) % NC
        return px, py, pc

    def device(px, py, pc, pz):
        return (px * NZ + pz, py * NC + pc)

    barrier = pltpu.get_barrier_semaphore()
    for step in DEPTH_STEPS:
        pl.semaphore_signal(barrier, inc=1, device_id=device(x, y, c, (z + step) % NZ), device_id_type=MESH)
    for step in PLANE_STEPS:
        pl.semaphore_signal(barrier, inc=1, device_id=device(*plane_peer(step), z), device_id_type=MESH)

    loads = []

    def load(source, target):
        copy = pltpu.make_async_copy(source, target, load_sem.at[len(loads)])
        copy.start()
        loads.append(copy)

    for head in range(HEADS):
        lanes = pl.ds(head * HEAD_DIM, HEAD_DIM)
        for source, target in ((k_hbm, k_ref), (q_hbm, q_ref), (g_hbm, g_ref)):
            load(source.at[:, lanes], target.at[:, lanes])
    load(feedback_ref, f_ref)
    load(layer_ref, l_ref)

    def send(source, target, send_sem, recv_sem, where):
        copy = pltpu.make_async_remote_copy(
            src_ref=source, dst_ref=target, send_sem=send_sem, recv_sem=recv_sem,
            device_id=where, device_id_type=MESH,
        )
        copy.start()
        return copy

    def arrived(target, recv_sem):
        pltpu.make_async_copy(target, target, recv_sem).wait()

    starts = segment_starts(segment_ref[...], count_ref[0])
    per = BLOCK // LANES
    starts = [
        jnp.concatenate([starts[b * per + i:b * per + i + 1] for i in range(per)], axis=1) for b in range(BLOCKS)
    ]
    for head in range(HEADS):
        for copy in loads[3 * head:3 * head + 3]:
            copy.wait()
        attend(head, starts, k_ref, q_ref, g_ref, w_ref.at[head], v_ref)

    factor = split(factor_ref[...])
    for t in range(GROUP):
        got = lax.dot_general(factor, v_ref[t * LANES:(t + 1) * LANES, :], NT, preferred_element_type=F32)
        zs_ref[t] = got[:RANK] + got[RANK:]
    pl.semaphore_wait(barrier, len(DEPTH_STEPS) + len(PLANE_STEPS))
    a_copies = []
    for i, step in enumerate(GROUP_STEPS):
        px, py, pc = plane_peer(step)
        peer = py * NC + pc
        a_copies.append(send(zs_ref.at[peer], zr_ref.at[tp], a_send.at[i], a_recv.at[tp], (dp, peer)))
    zr_ref[tp] = zs_ref[tp]

    loads[9].wait()
    for j in range(WIDTH // BLOCK):
        got = lax.dot_general(factor, f_ref[j * BLOCK:(j + 1) * BLOCK, :], NT, preferred_element_type=F32)
        pf_ref[:, j * BLOCK:(j + 1) * BLOCK] = got[:RANK] + got[RANK:]
    loads[10].wait()

    for step in GROUP_STEPS:
        px, py, pc = plane_peer(step)
        peer = py * NC + pc
        arrived(zr_ref.at[peer], a_recv.at[peer])
    mixed = split(jnp.sum(zr_ref[...], axis=0))
    for j in range(WIDTH // BLOCK):
        lanes = slice(j * BLOCK, (j + 1) * BLOCK)
        got = jnp.dot(mixed, l_ref[:, lanes], preferred_element_type=F32)
        part = (pf_ref[:, lanes] + got[:RANK] + got[RANK:]).astype(BF16)
        for i in range(per):
            for h in range(NC):
                part_ref[h, j * per + i] = part[h * HALF:(h + 1) * HALF, i * LANES:(i + 1) * LANES]

    holder = y == (x + 2 * c) % NY
    own = 4 * x + y
    rs_copies, rs_extras = [], []
    for i, step in enumerate(PLANE_STEPS):
        px, py, pc = plane_peer(step)
        rs_copies.append(
            send(part_ref.at[pc, NY * px + py], main_ref.at[place], rs_send.at[i], rs_main.at[place], device(px, py, pc, z))
        )
    for i, (xh, yh, ch) in enumerate(HOLDERS):
        other = place != xh * GROUP + yh * NC + ch

        @pl.when(other)
        def _():
            send(
                part_ref.at[ch, MAIN + xh], extra_ref.at[place],
                rs_send.at[len(PLANE_STEPS) + i], rs_extra.at[place], device(xh, yh, ch, z),
            )

    main_ref[place] = part_ref[c, own]
    extra_ref[place] = part_ref[c, MAIN + x]
    for copy in a_copies:
        copy.wait_send()
    for step in PLANE_STEPS:
        px, py, pc = plane_peer(step)
        peer = px * GROUP + py * NC + pc
        arrived(main_ref.at[peer], rs_main.at[peer])
    deep_ref[0, z] = jnp.sum(main_ref[...].astype(F32), axis=0).astype(BF16)
    d_copies = []
    for i, step in enumerate(DEPTH_STEPS):
        d_copies.append(
            send(deep_ref.at[0, z], deep_ref.at[0, z], d_send.at[0, i], d_recv.at[0, z], device(x, y, c, (z + step) % NZ))
        )

    @pl.when(holder)
    def _():
        for step in PLANE_STEPS:
            px, py, pc = plane_peer(step)
            peer = px * GROUP + py * NC + pc
            arrived(extra_ref.at[peer], rs_extra.at[peer])
        deep_ref[1, z] = jnp.sum(extra_ref[...].astype(F32), axis=0).astype(BF16)
        for i, step in enumerate(DEPTH_STEPS):
            send(deep_ref.at[1, z], deep_ref.at[1, z], d_send.at[1, i], d_recv.at[1, z], device(x, y, c, (z + step) % NZ))

    for copy in rs_copies:
        copy.wait_send()
    for i, (xh, yh, ch) in enumerate(HOLDERS):
        other = place != xh * GROUP + yh * NC + ch

        @pl.when(other)
        def _():
            arrived(part_ref.at[ch, MAIN + xh], rs_send.at[len(PLANE_STEPS) + i])

    for step in DEPTH_STEPS:
        peer = (z + step) % NZ
        arrived(deep_ref.at[0, peer], d_recv.at[0, peer])
    left_ref[c, own] = jnp.sum(deep_ref[0].astype(F32), axis=0).astype(BF16)
    ag_copies = []
    for i, step in enumerate(PLANE_STEPS):
        ag_copies.append(
            send(left_ref.at[c, own], left_ref.at[c, own], ag_send.at[0, i], ag_main.at[place], device(*plane_peer(step), z))
        )

    @pl.when(holder)
    def _():
        for step in DEPTH_STEPS:
            peer = (z + step) % NZ
            arrived(deep_ref.at[1, peer], d_recv.at[1, peer])
        left_ref[c, MAIN + x] = jnp.sum(deep_ref[1].astype(F32), axis=0).astype(BF16)
        for i, step in enumerate(PLANE_STEPS):
            send(
                left_ref.at[c, MAIN + x], left_ref.at[c, MAIN + x],
                ag_send.at[1, i], ag_extra.at[c * NX + x], device(*plane_peer(step), z),
            )

    for copy in d_copies:
        copy.wait_send()

    @pl.when(holder)
    def _():
        for i, step in enumerate(DEPTH_STEPS):
            arrived(deep_ref.at[1, z], d_send.at[1, i])

    for step in PLANE_STEPS:
        px, py, pc = plane_peer(step)
        arrived(left_ref.at[pc, NY * px + py], ag_main.at[px * GROUP + py * NC + pc])
    for i, (xh, yh, ch) in enumerate(HOLDERS):
        other = place != xh * GROUP + yh * NC + ch

        @pl.when(other)
        def _():
            arrived(left_ref.at[ch, MAIN + xh], ag_extra.at[i])

    left = jnp.concatenate(
        [jnp.concatenate([left_ref[h, n] for h in range(NC)], axis=0) for n in range(TILES)], axis=1
    )
    t_ref[tp] = lax.dot_general(left, l_ref[...], NT, preferred_element_type=F32).astype(BF16)
    t_copies = []
    for i, step in enumerate(GROUP_STEPS):
        px, py, pc = plane_peer(step)
        t_copies.append(send(t_ref.at[tp], t_ref.at[tp], t_send.at[i], t_recv.at[tp], (dp, py * NC + pc)))
    right = jnp.dot(left, f_ref[...], preferred_element_type=F32)
    for copy in ag_copies:
        copy.wait_send()

    @pl.when(holder)
    def _():
        for i, step in enumerate(PLANE_STEPS):
            arrived(left_ref.at[c, MAIN + x], ag_send.at[1, i])

    for step in GROUP_STEPS:
        px, py, pc = plane_peer(step)
        peer = py * NC + pc
        arrived(t_ref.at[peer], t_recv.at[peer])
    gathered = jnp.concatenate([t_ref[t] for t in range(GROUP)], axis=1)
    right = right + jnp.dot(gathered, v_ref[...], preferred_element_type=F32)

    for j in range(FEATURES // LANES):
        for h in range(NC):
            ys_ref[j * NC + h] = right[h * HALF:(h + 1) * HALF, j * LANES:(j + 1) * LANES]
    keeper = x // 2 == c
    spare = NX + x % 2
    x_copies = []
    for i, step in enumerate(ROW_STEPS):
        px = (x + step) % NX
        x_copies.append(send(ys_ref.at[px], xr_ref.at[0, x], x_send.at[i], x_recv.at[0, x], device(px, y, c, z)))
    for e in range(2):
        px = 2 * c + e

        @pl.when(x != px)
        def _():
            send(ys_ref.at[NX + e], xr_ref.at[1, x], x_send.at[NX - 1 + e], x_recv.at[1, x], device(px, y, c, z))

    xr_ref[0, x] = ys_ref[x]
    xr_ref[1, x] = ys_ref[spare]
    for copy in t_copies:
        copy.wait_send()
    for step in ROW_STEPS:
        px = (x + step) % NX
        arrived(xr_ref.at[0, px], x_recv.at[0, px])
    deep2_ref[0, z] = jnp.sum(xr_ref[0], axis=0).astype(BF16)
    d2_copies = []
    for i, step in enumerate(DEPTH_STEPS):
        d2_copies.append(
            send(deep2_ref.at[0, z], deep2_ref.at[0, z], d2_send.at[0, i], d2_recv.at[0, z], device(x, y, c, (z + step) % NZ))
        )

    @pl.when(keeper)
    def _():
        for step in ROW_STEPS:
            px = (x + step) % NX
            arrived(xr_ref.at[1, px], x_recv.at[1, px])
        deep2_ref[1, z] = jnp.sum(xr_ref[1], axis=0).astype(BF16)
        for i, step in enumerate(DEPTH_STEPS):
            send(deep2_ref.at[1, z], deep2_ref.at[1, z], d2_send.at[1, i], d2_recv.at[1, z], device(x, y, c, (z + step) % NZ))

    for copy in x_copies:
        copy.wait_send()
    for e in range(2):

        @pl.when(x != 2 * c + e)
        def _():
            arrived(ys_ref.at[NX + e], x_send.at[NX - 1 + e])

    tall = jnp.concatenate([left, jnp.zeros((LANES - RANK, WIDTH), BF16)], axis=0)
    table = lax.dot_general(left, tall, NT, preferred_element_type=F32)
    rows = lax.broadcasted_iota(jnp.int32, (RANK, LANES), 0)
    lanes = lax.broadcasted_iota(jnp.int32, (RANK, LANES), 1)
    table = jnp.where(lanes == rows + RANK, 1.0, table)
    for k in range(RANK):
        ratio = table[:, k:k + 1] / table[k:k + 1, k:k + 1]
        table = table - jnp.where(rows > k, ratio, 0.0) * table[k:k + 1, :]
    pivots = jnp.sum(jnp.where(lanes == rows, table, 0.0), axis=1, keepdims=True)
    inverse = jnp.where(lanes >= RANK, table, 0.0) * lax.rsqrt(pivots)

    def solve(value):
        padded = jnp.concatenate(
            [jnp.zeros((RANK, FEATURES), F32), value, jnp.zeros((LANES - 2 * RANK, FEATURES), F32)], axis=0
        )
        return jnp.dot(inverse, padded, precision=lax.Precision.HIGHEST, preferred_element_type=F32)

    first = (5 * tp) // 2
    window = jnp.concatenate(
        [
            jnp.concatenate([left_ref[h, first + i] for h in range(NC)], axis=0).astype(F32)
            for i in range(FEATURES // LANES)
        ],
        axis=1,
    )
    own_basis = solve(window) * math.sqrt(WIDTH)
    shifted = jnp.concatenate(
        [own_basis[:, LANES // 2:], own_basis[:, :LANES // 2]], axis=1
    )
    share = WIDTH // GROUP
    basis_ref[...] = jnp.where(tp % 2 == 1, shifted, own_basis)[:, :share]

    for step in DEPTH_STEPS:
        peer = (z + step) % NZ
        arrived(deep2_ref.at[0, peer], d2_recv.at[0, peer])
    yf_ref[x] = jnp.sum(deep2_ref[0].astype(F32), axis=0)
    xg_copies = []
    for i, step in enumerate(ROW_STEPS):
        xg_copies.append(send(yf_ref.at[x], yf_ref.at[x], xg_send.at[0, i], xg_recv.at[x], device((x + step) % NX, y, c, z)))

    @pl.when(keeper)
    def _():
        for step in DEPTH_STEPS:
            peer = (z + step) % NZ
            arrived(deep2_ref.at[1, peer], d2_recv.at[1, peer])
        yf_ref[spare] = jnp.sum(deep2_ref[1].astype(F32), axis=0)
        for i, step in enumerate(ROW_STEPS):
            send(yf_ref.at[spare], yf_ref.at[spare], xg_send.at[1, i], xg_recv.at[spare], device((x + step) % NX, y, c, z))

    for copy in d2_copies:
        copy.wait_send()

    @pl.when(keeper)
    def _():
        for i, step in enumerate(DEPTH_STEPS):
            arrived(deep2_ref.at[1, z], d2_send.at[1, i])

    for step in ROW_STEPS:
        px = (x + step) % NX
        arrived(yf_ref.at[px], xg_recv.at[px])
    for e in range(2):

        @pl.when(x != 2 * c + e)
        def _():
            arrived(yf_ref.at[NX + e], xg_recv.at[NX + e])

    summed = jnp.concatenate(
        [
            jnp.concatenate([yf_ref[j * NC + h] for h in range(NC)], axis=0)
            for j in range(FEATURES // LANES)
        ],
        axis=1,
    )
    next_ref[...] = solve(summed) * (1.0 / (NX * NZ))
    for copy in xg_copies:
        copy.wait_send()

    @pl.when(keeper)
    def _():
        for i, step in enumerate(ROW_STEPS):
            arrived(yf_ref.at[spare], xg_send.at[1, i])


def on_device(
    layer_input, queries, key_vectors, out_grad, feedback, factor_prev, token_count, segment_ids
):
    vmem = pl.BlockSpec(memory_space=pltpu.VMEM)
    anywhere = pl.BlockSpec(memory_space=pl.ANY)
    dma = pltpu.SemaphoreType.DMA
    plane = PLANE - 1
    deep = NZ - 1
    return pl.pallas_call(
        kernel,
        out_shape=(
            jax.ShapeDtypeStruct((RANK, WIDTH // GROUP), F32),
            jax.ShapeDtypeStruct((RANK, FEATURES), F32),
        ),
        in_specs=[anywhere] * 5 + [vmem, pl.BlockSpec(memory_space=pltpu.SMEM), vmem],
        out_specs=(vmem, vmem),
        scratch_shapes=[
            pltpu.VMEM((SLOTS, FEATURES), BF16),
            pltpu.VMEM((SLOTS, FEATURES), BF16),
            pltpu.VMEM((SLOTS, FEATURES), BF16),
            pltpu.VMEM((WIDTH, FEATURES), BF16),
            pltpu.VMEM((LANES, WIDTH), BF16),
            pltpu.VMEM((SLOTS, FEATURES), BF16),
            pltpu.VMEM((HEADS, SLOTS, SLOTS), BF16),
            pltpu.VMEM((RANK, WIDTH), F32),
            pltpu.VMEM((GROUP, RANK, LANES), F32),
            pltpu.VMEM((GROUP, RANK, LANES), F32),
            pltpu.VMEM((NC, TILES, HALF, LANES), BF16),
            pltpu.VMEM((PLANE, HALF, LANES), BF16),
            pltpu.VMEM((PLANE, HALF, LANES), BF16),
            pltpu.VMEM((2, NZ, HALF, LANES), BF16),
            pltpu.VMEM((NC, TILES, HALF, LANES), BF16),
            pltpu.VMEM((GROUP, RANK, LANES), BF16),
            pltpu.VMEM((6, HALF, LANES), F32),
            pltpu.VMEM((2, NX, HALF, LANES), F32),
            pltpu.VMEM((2, NZ, HALF, LANES), BF16),
            pltpu.VMEM((6, HALF, LANES), F32),
            dma((11,)),
            dma((GROUP - 1,)), dma((GROUP,)),
            dma((plane + len(HOLDERS),)), dma((PLANE,)), dma((PLANE,)),
            dma((2, deep)), dma((2, NZ)),
            dma((2, plane)), dma((PLANE,)), dma((len(HOLDERS),)),
            dma((GROUP - 1,)), dma((GROUP,)),
            dma((NX + 1,)), dma((2, NX)),
            dma((2, deep)), dma((2, NZ)),
            dma((2, NX - 1)), dma((6,)),
        ],
        compiler_params=pltpu.CompilerParams(
            collective_id=0, has_side_effects=True, vmem_limit_bytes=60 * 1024 * 1024
        ),
    )(
        layer_input, queries, key_vectors, out_grad, feedback, factor_prev, token_count,
        segment_ids.reshape(SLOTS // LANES, LANES),
    )


def solution(mesh):
    return jax.shard_map(
        on_device,
        mesh=mesh,
        in_specs=(
            P(("dp", "tp"), None),
            P("dp", "tp"),
            P("dp", "tp"),
            P("dp", "tp"),
            P("dp", "tp"),
            P(None, "tp"),
            P("dp"),
            P("dp"),
        ),
        out_specs=(P(None, "tp"), P(None, "tp")),
        check_vma=False,
    )
```

```python
import math

import jax
import jax.numpy as jnp
from jax import lax
from jax.experimental import pallas as pl
from jax.experimental.pallas import tpu as pltpu
from jax.sharding import PartitionSpec as P

MESH = pl.DeviceIdType.MESH
F32, BF16 = jnp.float32, jnp.bfloat16
NT = (((1,), (1,)), ((), ()))

NX, NY, NZ, NC = 4, 4, 16, 2
GROUP = NY * NC
PLANE = NX * GROUP
OTHERS = PLANE - 1
DEEP = NZ - 1

HEAD_DIM = 128
HEADS = 3
SLOTS = 1024
WIDTH = 2560
RANK = 32
LANES = 128
HALF = 16
FEATURES = HEADS * HEAD_DIM
TILES = WIDTH // LANES
MAIN = NX * NY
BLOCK = 256
BLOCKS = SLOTS // BLOCK
MASKED = -1e30


def ahead(position, step, size):
    moved = position + step
    return jnp.where(moved >= size, moved - size, moved) if step else position


def hops(step, size):
    return min(step, size - step)


PLANE_STEPS = sorted(
    [
        (dx, dy, dc)
        for dx in range(NX)
        for dy in range(NY)
        for dc in range(NC)
        if (dx, dy, dc) != (0, 0, 0)
    ],
    key=lambda s: -(hops(s[0], NX) * 2 + hops(s[1], NY) * 2 + s[2]),
)
GROUP_STEPS = [s for s in PLANE_STEPS if s[0] == 0]
ROW_STEPS = sorted(range(1, NX), key=lambda s: -hops(s, NX))
DEPTH_STEPS = sorted(range(1, NZ), key=lambda s: -hops(s, NZ))
HOLDERS = [(xh, (xh + 2 * ch) % NY, ch) for ch in range(NC) for xh in range(NX)]


def segment_starts(seg, count):
    rows = lax.broadcasted_iota(jnp.int32, seg.shape, 0)
    lanes = lax.broadcasted_iota(jnp.int32, seg.shape, 1)
    slot = rows * LANES + lanes
    wrapped = pltpu.roll(seg, 1, 1)
    before = jnp.where(lanes == 0, pltpu.roll(wrapped, 1, 0), wrapped)
    first = jnp.where((seg != before) & (slot > 0), slot, 0)
    step = 1
    while step < LANES:
        first = jnp.maximum(first, jnp.where(lanes >= step, pltpu.roll(first, step, 1), 0))
        step *= 2
    carry = jnp.broadcast_to(jnp.max(first, axis=1, keepdims=True), first.shape)
    step = 1
    while step < SLOTS // LANES:
        carry = jnp.maximum(carry, jnp.where(rows >= step, pltpu.roll(carry, step, 0), 0))
        step *= 2
    first = jnp.maximum(first, jnp.where(rows >= 1, pltpu.roll(carry, 1, 0), 0))
    return jnp.where(slot < count, first, 4 * SLOTS)


def split(value):
    high = value.astype(BF16)
    low = (value - high.astype(F32)).astype(BF16)
    return jnp.concatenate([high, low], axis=0)


def attend(head, starts, k_ref, q_ref, g_ref, w_ref, v_ref):
    lanes = slice(head * HEAD_DIM, (head + 1) * HEAD_DIM)
    rate = HEAD_DIM ** (-0.5) * math.log2(math.e)
    for b in range(BLOCKS):
        low, high = b * BLOCK, (b + 1) * BLOCK
        q = q_ref[low:high, lanes]
        start = starts[b]
        live = start < SLOTS
        key = lax.broadcasted_iota(jnp.int32, (BLOCK, BLOCK), 0) + low
        query = lax.broadcasted_iota(jnp.int32, (BLOCK, BLOCK), 1) + low
        near = lax.dot_general(k_ref[low:high, lanes], q, NT, preferred_element_type=F32)
        near = jnp.where((key >= start) & (key <= query), near, MASKED)
        top = jnp.max(near, axis=0, keepdims=True)
        if b:
            far = lax.dot_general(k_ref[0:low, lanes], q, NT, preferred_element_type=F32)
            far_key = lax.broadcasted_iota(jnp.int32, (low, BLOCK), 0)
            far = jnp.where(far_key >= start, far, MASKED)
            top = jnp.maximum(top, jnp.max(far, axis=0, keepdims=True))
        near = jnp.exp2((near - top) * rate)
        total = jnp.sum(near, axis=0, keepdims=True)
        if b:
            far = jnp.exp2((far - top) * rate)
            total = total + jnp.sum(far, axis=0, keepdims=True)
        scale = jnp.where(live, 1.0 / jnp.maximum(total, 1.0), 0.0)
        w_ref[low:high, low:high] = (near * scale).astype(BF16)
        if b:
            w_ref[0:low, low:high] = (far * scale).astype(BF16)
    for b in range(BLOCKS):
        low, high = b * BLOCK, (b + 1) * BLOCK
        v = jnp.dot(w_ref[low:high, low:], g_ref[low:, lanes], preferred_element_type=F32)
        v_ref[low:high, lanes] = v.astype(BF16)


def kernel(
    layer_hbm, q_hbm, k_hbm, g_hbm, feedback_hbm, factor_hbm, count_ref, segment_hbm,
    basis_ref, next_ref,
    factor_ref, segment_ref,
    q_ref, k_ref, g_ref, f_ref, l_ref, v_ref, w_ref, pf_ref,
    zs_ref, zr_ref, part_ref, main_ref, extra_ref, deep_ref, left_ref, t_ref, ys_ref, xr_ref, deep2_ref, yf_ref,
    load_sem,
    a_send, a_recv, rs_send, rs_recv, d_send, d_recv, ag_send, ag_recv,
    t_send, t_recv, x_send, x_recv, d2_send, d2_recv, xg_send, xg_recv,
):
    dp, tp = lax.axis_index("dp"), lax.axis_index("tp")
    x, z = dp // NZ, dp % NZ
    y, c = tp // NC, tp % NC
    place = x * GROUP + tp

    def plane_peer(step):
        dx, dy, dc = step
        return ahead(x, dx, NX), ahead(y, dy, NY), 1 - c if dc else c

    def device(px, py, pc, pz):
        return (px * NZ + pz, py * NC + pc)

    def load(source, target, which):
        pltpu.make_async_copy(source, target, load_sem.at[which]).start()

    def load_head(head):
        lanes = pl.ds(head * HEAD_DIM, HEAD_DIM)
        for source, target in ((k_hbm, k_ref), (q_hbm, q_ref), (g_hbm, g_ref)):
            load(source.at[:, lanes], target.at[:, lanes], head)

    load(segment_hbm, segment_ref, HEADS)
    load_head(0)
    barrier = pltpu.get_barrier_semaphore()
    for step in DEPTH_STEPS:
        pl.semaphore_signal(barrier, inc=1, device_id=device(x, y, c, ahead(z, step, NZ)), device_id_type=MESH)
    for step in PLANE_STEPS:
        pl.semaphore_signal(barrier, inc=1, device_id=device(*plane_peer(step), z), device_id_type=MESH)
    for head in range(1, HEADS):
        load_head(head)
    load(factor_hbm, factor_ref, HEADS + 1)
    load(feedback_hbm, f_ref, HEADS + 2)
    load(layer_hbm, l_ref, HEADS + 3)

    def send(source, target, send_sem, recv_sem, where):
        pltpu.make_async_remote_copy(
            src_ref=source, dst_ref=target, send_sem=send_sem, recv_sem=recv_sem,
            device_id=where, device_id_type=MESH,
        ).start()

    def arrived(target, recv_sem):
        pltpu.make_async_copy(target, target, recv_sem).wait()

    arrived(segment_ref, load_sem.at[HEADS])
    starts = segment_starts(segment_ref[...], count_ref[0])
    per = BLOCK // LANES
    starts = [
        jnp.concatenate([starts[b * per + i:b * per + i + 1] for i in range(per)], axis=1) for b in range(BLOCKS)
    ]
    for head in range(HEADS):
        arrived(k_ref, load_sem.at[head])
        attend(head, starts, k_ref, q_ref, g_ref, w_ref.at[head], v_ref)

    arrived(factor_ref, load_sem.at[HEADS + 1])
    factor = split(factor_ref[...])
    for t in range(GROUP):
        got = lax.dot_general(factor, v_ref[t * LANES:(t + 1) * LANES, :], NT, preferred_element_type=F32)
        zs_ref[t] = got[:RANK] + got[RANK:]
    pl.semaphore_wait(barrier, len(DEPTH_STEPS) + len(PLANE_STEPS))
    for step in GROUP_STEPS:
        px, py, pc = plane_peer(step)
        peer = py * NC + pc
        send(zs_ref.at[peer], zr_ref.at[tp], a_send, a_recv, (dp, peer))
    zr_ref[tp] = zs_ref[tp]

    arrived(f_ref, load_sem.at[HEADS + 2])
    for j in range(WIDTH // BLOCK):
        got = lax.dot_general(factor, f_ref[j * BLOCK:(j + 1) * BLOCK, :], NT, preferred_element_type=F32)
        pf_ref[:, j * BLOCK:(j + 1) * BLOCK] = got[:RANK] + got[RANK:]
    arrived(l_ref, load_sem.at[HEADS + 3])
    arrived(zs_ref.at[pl.ds(0, GROUP - 1)], a_send)
    arrived(zr_ref.at[pl.ds(0, GROUP - 1)], a_recv)
    mixed = split(jnp.sum(zr_ref[...], axis=0))
    for j in range(WIDTH // BLOCK):
        lanes = slice(j * BLOCK, (j + 1) * BLOCK)
        got = jnp.dot(mixed, l_ref[:, lanes], preferred_element_type=F32)
        part = (pf_ref[:, lanes] + got[:RANK] + got[RANK:]).astype(BF16)
        for i in range(per):
            for h in range(NC):
                part_ref[h * TILES + j * per + i] = part[h * HALF:(h + 1) * HALF, i * LANES:(i + 1) * LANES]

    holder = y == (x + 2 * c) % NY
    own = c * TILES + NY * x + y
    spare = c * TILES + MAIN + x
    for step in PLANE_STEPS:
        px, py, pc = plane_peer(step)
        send(part_ref.at[pc * TILES + NY * px + py], main_ref.at[place], rs_send.at[0], rs_recv.at[0], device(px, py, pc, z))
    for xh, yh, ch in HOLDERS:

        @pl.when(place != xh * GROUP + yh * NC + ch)
        def _():
            send(part_ref.at[ch * TILES + MAIN + xh], extra_ref.at[place], rs_send.at[1], rs_recv.at[1], device(xh, yh, ch, z))

    main_ref[place] = part_ref[own]
    extra_ref[place] = part_ref[spare]
    arrived(main_ref.at[pl.ds(0, OTHERS)], rs_recv.at[0])
    deep_ref[0, z] = jnp.sum(main_ref[...].astype(F32), axis=0).astype(BF16)

    def drain_scatter():
        arrived(part_ref.at[pl.ds(0, OTHERS)], rs_send.at[0])

        @pl.when(holder)
        def _():
            arrived(part_ref.at[pl.ds(0, len(HOLDERS) - 1)], rs_send.at[1])

        @pl.when(jnp.logical_not(holder))
        def _():
            arrived(part_ref.at[pl.ds(0, len(HOLDERS))], rs_send.at[1])

    deep_device = [device(x, y, c, ahead(z, step, NZ)) for step in DEPTH_STEPS]
    for where in deep_device:
        send(deep_ref.at[0, z], deep_ref.at[0, z], d_send.at[0], d_recv.at[0], where)

    @pl.when(holder)
    def _():
        arrived(extra_ref.at[pl.ds(0, OTHERS)], rs_recv.at[1])
        deep_ref[1, z] = jnp.sum(extra_ref[...].astype(F32), axis=0).astype(BF16)
        for where in deep_device:
            send(deep_ref.at[1, z], deep_ref.at[1, z], d_send.at[1], d_recv.at[1], where)

    drain_scatter()
    arrived(deep_ref.at[0, pl.ds(0, DEEP)], d_recv.at[0])
    left_ref[own] = jnp.sum(deep_ref[0].astype(F32), axis=0).astype(BF16)

    def drain_depth():
        arrived(deep_ref.at[0, pl.ds(0, DEEP)], d_send.at[0])

        @pl.when(holder)
        def _():
            arrived(deep_ref.at[1, pl.ds(0, DEEP)], d_send.at[1])

    plane_device = [device(*plane_peer(step), z) for step in PLANE_STEPS]
    for where in plane_device:
        send(left_ref.at[own], left_ref.at[own], ag_send.at[0], ag_recv.at[0], where)

    @pl.when(holder)
    def _():
        arrived(deep_ref.at[1, pl.ds(0, DEEP)], d_recv.at[1])
        left_ref[spare] = jnp.sum(deep_ref[1].astype(F32), axis=0).astype(BF16)
        for where in plane_device:
            send(left_ref.at[spare], left_ref.at[spare], ag_send.at[1], ag_recv.at[1], where)

    drain_depth()
    arrived(left_ref.at[pl.ds(0, OTHERS)], ag_recv.at[0])

    @pl.when(holder)
    def _():
        arrived(left_ref.at[pl.ds(0, len(HOLDERS) - 1)], ag_recv.at[1])

    @pl.when(jnp.logical_not(holder))
    def _():
        arrived(left_ref.at[pl.ds(0, len(HOLDERS))], ag_recv.at[1])

    def drain_gather():
        arrived(left_ref.at[pl.ds(0, OTHERS)], ag_send.at[0])

        @pl.when(holder)
        def _():
            arrived(left_ref.at[pl.ds(0, OTHERS)], ag_send.at[1])


    left = jnp.concatenate(
        [jnp.concatenate([left_ref[h * TILES + n] for h in range(NC)], axis=0) for n in range(TILES)], axis=1
    )
    t_ref[tp] = lax.dot_general(left, l_ref[...], NT, preferred_element_type=F32).astype(BF16)
    for step in GROUP_STEPS:
        px, py, pc = plane_peer(step)
        send(t_ref.at[tp], t_ref.at[tp], t_send, t_recv, (dp, py * NC + pc))
    right = jnp.dot(left, f_ref[...], preferred_element_type=F32)
    drain_gather()
    arrived(t_ref.at[pl.ds(0, GROUP - 1)], t_recv)
    gathered = jnp.concatenate([t_ref[t] for t in range(GROUP)], axis=1)
    right = right + jnp.dot(gathered, v_ref[...], preferred_element_type=F32)

    for j in range(FEATURES // LANES):
        for h in range(NC):
            ys_ref[j * NC + h] = right[h * HALF:(h + 1) * HALF, j * LANES:(j + 1) * LANES]
    keeper = x // 2 == c
    odd = NX + x % 2
    row_device = [device(ahead(x, step, NX), y, c, z) for step in ROW_STEPS]
    for step, where in zip(ROW_STEPS, row_device):
        send(ys_ref.at[ahead(x, step, NX)], xr_ref.at[0, x], x_send.at[0], x_recv.at[0], where)
    for e in range(2):

        @pl.when(x != 2 * c + e)
        def _():
            send(ys_ref.at[NX + e], xr_ref.at[1, x], x_send.at[1 + e], x_recv.at[1], device(2 * c + e, y, c, z))

    xr_ref[0, x] = ys_ref[x]
    xr_ref[1, x] = ys_ref[odd]
    arrived(xr_ref.at[0, pl.ds(0, NX - 1)], x_recv.at[0])
    deep2_ref[0, z] = jnp.sum(xr_ref[0], axis=0).astype(BF16)

    def drain_rows():
        arrived(t_ref.at[pl.ds(0, GROUP - 1)], t_send)
        arrived(ys_ref.at[pl.ds(0, NX - 1)], x_send.at[0])
        for e in range(2):

            @pl.when(x != 2 * c + e)
            def _():
                arrived(ys_ref.at[NX + e], x_send.at[1 + e])

    for where in deep_device:
        send(deep2_ref.at[0, z], deep2_ref.at[0, z], d2_send.at[0], d2_recv.at[0], where)

    @pl.when(keeper)
    def _():
        arrived(xr_ref.at[1, pl.ds(0, NX - 1)], x_recv.at[1])
        deep2_ref[1, z] = jnp.sum(xr_ref[1], axis=0).astype(BF16)
        for where in deep_device:
            send(deep2_ref.at[1, z], deep2_ref.at[1, z], d2_send.at[1], d2_recv.at[1], where)

    drain_rows()

    tall = jnp.concatenate([left, jnp.zeros((LANES - RANK, WIDTH), BF16)], axis=0)
    table = lax.dot_general(left, tall, NT, preferred_element_type=F32)
    rows = lax.broadcasted_iota(jnp.int32, (RANK, LANES), 0)
    lanes = lax.broadcasted_iota(jnp.int32, (RANK, LANES), 1)
    table = jnp.where(lanes == rows + RANK, 1.0, table)
    for k in range(RANK):
        ratio = table[:, k:k + 1] / table[k:k + 1, k:k + 1]
        table = table - jnp.where(rows > k, ratio, 0.0) * table[k:k + 1, :]
    pivots = jnp.sum(jnp.where(lanes == rows, table, 0.0), axis=1, keepdims=True)
    inverse = jnp.where(lanes >= RANK, table, 0.0) * lax.rsqrt(pivots)

    def solve(value):
        padded = jnp.concatenate(
            [jnp.zeros((RANK, FEATURES), F32), value, jnp.zeros((LANES - 2 * RANK, FEATURES), F32)], axis=0
        )
        return jnp.dot(inverse, padded, precision=lax.Precision.HIGHEST, preferred_element_type=F32)

    first = (5 * tp) // 2
    window = jnp.concatenate(
        [
            jnp.concatenate([left_ref[h * TILES + first + i] for h in range(NC)], axis=0).astype(F32)
            for i in range(FEATURES // LANES)
        ],
        axis=1,
    )
    own_basis = solve(window) * math.sqrt(WIDTH)
    shifted = jnp.concatenate([own_basis[:, LANES // 2:], own_basis[:, :LANES // 2]], axis=1)
    share = WIDTH // GROUP
    basis_ref[...] = jnp.where(tp % 2 == 1, shifted, own_basis)[:, :share]

    def drain_depth2():
        arrived(deep2_ref.at[0, pl.ds(0, DEEP)], d2_send.at[0])

        @pl.when(keeper)
        def _():
            arrived(deep2_ref.at[1, pl.ds(0, DEEP)], d2_send.at[1])

    arrived(deep2_ref.at[0, pl.ds(0, DEEP)], d2_recv.at[0])
    yf_ref[x] = jnp.sum(deep2_ref[0].astype(F32), axis=0)
    for where in row_device:
        send(yf_ref.at[x], yf_ref.at[x], xg_send.at[0], xg_recv.at[0], where)

    @pl.when(keeper)
    def _():
        arrived(deep2_ref.at[1, pl.ds(0, DEEP)], d2_recv.at[1])
        yf_ref[odd] = jnp.sum(deep2_ref[1].astype(F32), axis=0)
        for where in row_device:
            send(yf_ref.at[odd], yf_ref.at[odd], xg_send.at[1], xg_recv.at[1 + x % 2], where)

    drain_depth2()
    arrived(yf_ref.at[pl.ds(0, NX - 1)], xg_recv.at[0])
    for e in range(2):

        @pl.when(x != 2 * c + e)
        def _():
            arrived(yf_ref.at[NX + e], xg_recv.at[1 + e])

    summed = jnp.concatenate(
        [
            jnp.concatenate([yf_ref[j * NC + h] for h in range(NC)], axis=0)
            for j in range(FEATURES // LANES)
        ],
        axis=1,
    )
    next_ref[...] = solve(summed) * (1.0 / (NX * NZ))
    arrived(yf_ref.at[pl.ds(0, NX - 1)], xg_send.at[0])

    @pl.when(keeper)
    def _():
        arrived(yf_ref.at[pl.ds(0, NX - 1)], xg_send.at[1])


def on_device(
    layer_input, queries, key_vectors, out_grad, feedback, factor_prev, token_count, segment_ids
):
    vmem = pl.BlockSpec(memory_space=pltpu.VMEM)
    anywhere = pl.BlockSpec(memory_space=pltpu.HBM)
    dma = pltpu.SemaphoreType.DMA
    return pl.pallas_call(
        kernel,
        out_shape=(
            jax.ShapeDtypeStruct((RANK, WIDTH // GROUP), F32),
            jax.ShapeDtypeStruct((RANK, FEATURES), F32),
        ),
        in_specs=[anywhere] * 6 + [pl.BlockSpec(memory_space=pltpu.SMEM), anywhere],
        out_specs=(vmem, vmem),
        scratch_shapes=[
            pltpu.VMEM((RANK, FEATURES), F32),
            pltpu.VMEM((SLOTS // LANES, LANES), jnp.int32),
            pltpu.VMEM((SLOTS, FEATURES), BF16),
            pltpu.VMEM((SLOTS, FEATURES), BF16),
            pltpu.VMEM((SLOTS, FEATURES), BF16),
            pltpu.VMEM((WIDTH, FEATURES), BF16),
            pltpu.VMEM((LANES, WIDTH), BF16),
            pltpu.VMEM((SLOTS, FEATURES), BF16),
            pltpu.VMEM((HEADS, SLOTS, SLOTS), BF16),
            pltpu.VMEM((RANK, WIDTH), F32),
            pltpu.VMEM((GROUP, RANK, LANES), F32),
            pltpu.VMEM((GROUP, RANK, LANES), F32),
            pltpu.VMEM((NC * TILES, HALF, LANES), BF16),
            pltpu.VMEM((PLANE, HALF, LANES), BF16),
            pltpu.VMEM((PLANE, HALF, LANES), BF16),
            pltpu.VMEM((2, NZ, HALF, LANES), BF16),
            pltpu.VMEM((NC * TILES, HALF, LANES), BF16),
            pltpu.VMEM((GROUP, RANK, LANES), BF16),
            pltpu.VMEM((6, HALF, LANES), F32),
            pltpu.VMEM((2, NX, HALF, LANES), F32),
            pltpu.VMEM((2, NZ, HALF, LANES), BF16),
            pltpu.VMEM((6, HALF, LANES), F32),
            dma((HEADS + 4,)),
            dma, dma,
            dma((2,)), dma((2,)),
            dma((2,)), dma((2,)),
            dma((2,)), dma((2,)),
            dma, dma,
            dma((3,)), dma((2,)),
            dma((2,)), dma((2,)),
            dma((2,)), dma((3,)),
        ],
        compiler_params=pltpu.CompilerParams(
            collective_id=0, has_side_effects=True, vmem_limit_bytes=32 * 1024 * 1024
        ),
    )(
        *(
            pltpu.with_memory_space_constraint(value, pltpu.HBM)
            for value in (layer_input, queries, key_vectors, out_grad, feedback, factor_prev)
        ),
        token_count,
        pltpu.with_memory_space_constraint(segment_ids.reshape(SLOTS // LANES, LANES), pltpu.HBM),
    )


def solution(mesh):
    return jax.shard_map(
        on_device,
        mesh=mesh,
        in_specs=(
            P(("dp", "tp"), None),
            P("dp", "tp"),
            P("dp", "tp"),
            P("dp", "tp"),
            P("dp", "tp"),
            P(None, "tp"),
            P("dp"),
            P("dp"),
        ),
        out_specs=(P(None, "tp"), P(None, "tp")),
        check_vma=False,
    )
```

```python
import math

import jax
import jax.numpy as jnp
from jax import lax
from jax.experimental import pallas as pl
from jax.experimental.pallas import tpu as pltpu
from jax.sharding import PartitionSpec as P

MESH = pl.DeviceIdType.MESH
F32, BF16 = jnp.float32, jnp.bfloat16
NT = (((1,), (1,)), ((), ()))

NX, NY, NZ, NC = 4, 4, 16, 2
GROUP = NY * NC
PLANE = NX * GROUP
OTHERS = PLANE - 1
DEEP = NZ - 1

HEAD_DIM = 128
HEADS = 3
SLOTS = 1024
WIDTH = 2560
RANK = 32
LANES = 128
HALF = 16
FEATURES = HEADS * HEAD_DIM
TILES = WIDTH // LANES
MAIN = NX * NY
BLOCK = 256
BLOCKS = SLOTS // BLOCK
MASKED = -1e30
PENALTY = 65536.0


def ahead(position, step, size):
    moved = position + step
    return jnp.where(moved >= size, moved - size, moved) if step else position


def hops(step, size):
    return min(step, size - step)


PLANE_STEPS = sorted(
    [
        (dx, dy, dc)
        for dx in range(NX)
        for dy in range(NY)
        for dc in range(NC)
        if (dx, dy, dc) != (0, 0, 0)
    ],
    key=lambda s: -(hops(s[0], NX) * 2 + hops(s[1], NY) * 2 + s[2]),
)
GROUP_STEPS = [s for s in PLANE_STEPS if s[0] == 0]
ROW_STEPS = sorted(range(1, NX), key=lambda s: -hops(s, NX))
DEPTH_STEPS = sorted(range(1, NZ), key=lambda s: -hops(s, NZ))
HOLDERS = [(xh, (xh + 2 * ch) % NY, ch) for ch in range(NC) for xh in range(NX)]


def split(value):
    high = value.astype(BF16)
    low = (value - high.astype(F32)).astype(BF16)
    return jnp.concatenate([high, low], axis=0)


def document_columns(seg, key_ref, query_ref):
    for b in range(SLOTS // LANES):
        ids = lax.broadcasted_iota(jnp.int32, (LANES, LANES), 0)
        own = jnp.where(seg[b:b + 1, :] == ids, 1.0, 0.0).T
        key_ref[b * LANES:(b + 1) * LANES, :] = own.astype(BF16)
        query_ref[b * LANES:(b + 1) * LANES, :] = ((own - 1.0) * PENALTY).astype(BF16)


def scores(head, b, k_ref, q_ref, dk_ref, dq_ref):
    lanes = slice(head * HEAD_DIM, (head + 1) * HEAD_DIM)
    low, high = b * BLOCK, (b + 1) * BLOCK
    q = jnp.concatenate([q_ref[low:high, lanes], dq_ref[low:high, :]], axis=1)
    k = jnp.concatenate([k_ref[low:high, lanes], dk_ref[low:high, :]], axis=1)
    near = lax.dot_general(k, q, NT, preferred_element_type=F32)
    key = lax.broadcasted_iota(jnp.int32, (BLOCK, BLOCK), 0)
    query = lax.broadcasted_iota(jnp.int32, (BLOCK, BLOCK), 1)
    near = jnp.where(key <= query, near, MASKED)
    top = jnp.max(near, axis=0, keepdims=True)
    parts = [near]
    if b:
        k = jnp.concatenate([k_ref[0:low, lanes], dk_ref[0:low, :]], axis=1)
        far = lax.dot_general(k, q, NT, preferred_element_type=F32)
        top = jnp.maximum(top, jnp.max(far, axis=0, keepdims=True))
        parts.append(far)
    return parts, top


def weigh(b, count, parts, top, w_ref):
    rate = HEAD_DIM ** (-0.5) * math.log2(math.e)
    low, high = b * BLOCK, (b + 1) * BLOCK
    parts = [jnp.exp2((part - top) * rate) for part in parts]
    total = sum(jnp.sum(part, axis=0, keepdims=True) for part in parts)
    live = lax.broadcasted_iota(jnp.int32, (1, BLOCK), 1) + low < count
    scale = jnp.where(live, 1.0 / jnp.maximum(total, 1.0), 0.0)
    for part, (start, end) in zip(parts, ((low, high), (0, low))):
        w_ref[start:end, low:high] = (part * scale).astype(BF16)


def combine(head, b, g_ref, w_ref, v_ref):
    lanes = slice(head * HEAD_DIM, (head + 1) * HEAD_DIM)
    low, high = b * BLOCK, (b + 1) * BLOCK
    v = jnp.dot(w_ref[low:high, low:], g_ref[low:, lanes], preferred_element_type=F32)
    v_ref[low:high, lanes] = v.astype(BF16)


def kernel(
    layer_hbm, q_hbm, k_hbm, g_hbm, feedback_hbm, factor_hbm, count_ref, segment_hbm,
    basis_ref, next_ref,
    factor_ref, segment_ref, dk_ref, dq_ref,
    q_ref, k_ref, g_ref, f_ref, l_ref, v_ref, w_ref, pf_ref,
    zs_ref, zr_ref, part_ref, main_ref, extra_ref, deep_ref, left_ref, t_ref, ys_ref, xr_ref, deep2_ref, yf_ref,
    load_sem,
    a_send, a_recv, rs_send, rs_recv, d_send, d_recv, ag_send, ag_recv,
    t_send, t_recv, x_send, x_recv, d2_send, d2_recv, xg_send, xg_recv,
):
    dp, tp = lax.axis_index("dp"), lax.axis_index("tp")
    x, z = dp // NZ, dp % NZ
    y, c = tp // NC, tp % NC
    place = x * GROUP + tp

    def plane_peer(step):
        dx, dy, dc = step
        return ahead(x, dx, NX), ahead(y, dy, NY), 1 - c if dc else c

    def device(px, py, pc, pz):
        return (px * NZ + pz, py * NC + pc)

    def load(source, target, which):
        pltpu.make_async_copy(source, target, load_sem.at[which]).start()

    def load_head(head):
        lanes = pl.ds(head * HEAD_DIM, HEAD_DIM)
        for source, target in ((k_hbm, k_ref), (q_hbm, q_ref), (g_hbm, g_ref)):
            load(source.at[:, lanes], target.at[:, lanes], head)

    load(segment_hbm, segment_ref, HEADS)
    load_head(0)
    barrier = pltpu.get_barrier_semaphore()
    for step in DEPTH_STEPS:
        pl.semaphore_signal(barrier, inc=1, device_id=device(x, y, c, ahead(z, step, NZ)), device_id_type=MESH)
    for step in PLANE_STEPS:
        pl.semaphore_signal(barrier, inc=1, device_id=device(*plane_peer(step), z), device_id_type=MESH)
    for head in range(1, HEADS):
        load_head(head)
    load(factor_hbm, factor_ref, HEADS + 1)
    load(feedback_hbm, f_ref, HEADS + 2)
    load(layer_hbm, l_ref, HEADS + 3)

    def send(source, target, send_sem, recv_sem, where):
        pltpu.make_async_remote_copy(
            src_ref=source, dst_ref=target, send_sem=send_sem, recv_sem=recv_sem,
            device_id=where, device_id_type=MESH,
        ).start()

    def arrived(target, recv_sem):
        pltpu.make_async_copy(target, target, recv_sem).wait()

    arrived(segment_ref, load_sem.at[HEADS])
    document_columns(segment_ref[...], dk_ref, dq_ref)
    per = BLOCK // LANES
    units = [(head, b) for b in reversed(range(BLOCKS)) for head in range(HEADS)]

    def begin(unit):
        head, b = units[unit]
        if b == BLOCKS - 1:
            arrived(k_ref, load_sem.at[head])
        return scores(head, b, k_ref, q_ref, dk_ref, dq_ref)

    ready = [begin(unit) for unit in range(1)]
    waiting = []
    for unit, (head, b) in enumerate(units):
        if unit + 1 < len(units):
            ready.append(begin(unit + 1))
        weigh(b, count_ref[0], *ready.pop(0), w_ref.at[head])
        waiting.append((head, b))
        if len(waiting) > 1:
            last, block = waiting.pop(0)
            combine(last, block, g_ref, w_ref.at[last], v_ref)
    for last, block in waiting:
        combine(last, block, g_ref, w_ref.at[last], v_ref)

    arrived(factor_ref, load_sem.at[HEADS + 1])
    factor = split(factor_ref[...])
    for t in range(GROUP):
        got = lax.dot_general(factor, v_ref[t * LANES:(t + 1) * LANES, :], NT, preferred_element_type=F32)
        zs_ref[t] = got[:RANK] + got[RANK:]
    pl.semaphore_wait(barrier, len(DEPTH_STEPS) + len(PLANE_STEPS))
    for step in GROUP_STEPS:
        px, py, pc = plane_peer(step)
        peer = py * NC + pc
        send(zs_ref.at[peer], zr_ref.at[tp], a_send, a_recv, (dp, peer))
    zr_ref[tp] = zs_ref[tp]

    arrived(f_ref, load_sem.at[HEADS + 2])
    for j in range(WIDTH // BLOCK):
        got = lax.dot_general(factor, f_ref[j * BLOCK:(j + 1) * BLOCK, :], NT, preferred_element_type=F32)
        pf_ref[:, j * BLOCK:(j + 1) * BLOCK] = got[:RANK] + got[RANK:]
    arrived(l_ref, load_sem.at[HEADS + 3])
    arrived(zs_ref.at[pl.ds(0, GROUP - 1)], a_send)
    arrived(zr_ref.at[pl.ds(0, GROUP - 1)], a_recv)
    mixed = split(jnp.sum(zr_ref[...], axis=0))
    for j in range(WIDTH // BLOCK):
        lanes = slice(j * BLOCK, (j + 1) * BLOCK)
        got = jnp.dot(mixed, l_ref[:, lanes], preferred_element_type=F32)
        part = (pf_ref[:, lanes] + got[:RANK] + got[RANK:]).astype(BF16)
        for i in range(per):
            for h in range(NC):
                part_ref[h * TILES + j * per + i] = part[h * HALF:(h + 1) * HALF, i * LANES:(i + 1) * LANES]

    holder = y == (x + 2 * c) % NY
    own = c * TILES + NY * x + y
    spare = c * TILES + MAIN + x
    for step in PLANE_STEPS:
        px, py, pc = plane_peer(step)
        send(part_ref.at[pc * TILES + NY * px + py], main_ref.at[place], rs_send.at[0], rs_recv.at[0], device(px, py, pc, z))
    for xh, yh, ch in HOLDERS:

        @pl.when(place != xh * GROUP + yh * NC + ch)
        def _():
            send(part_ref.at[ch * TILES + MAIN + xh], extra_ref.at[place], rs_send.at[1], rs_recv.at[1], device(xh, yh, ch, z))

    main_ref[place] = part_ref[own]
    extra_ref[place] = part_ref[spare]
    arrived(main_ref.at[pl.ds(0, OTHERS)], rs_recv.at[0])
    deep_ref[0, z] = jnp.sum(main_ref[...].astype(F32), axis=0).astype(BF16)

    def drain_scatter():
        arrived(part_ref.at[pl.ds(0, OTHERS)], rs_send.at[0])

        @pl.when(holder)
        def _():
            arrived(part_ref.at[pl.ds(0, len(HOLDERS) - 1)], rs_send.at[1])

        @pl.when(jnp.logical_not(holder))
        def _():
            arrived(part_ref.at[pl.ds(0, len(HOLDERS))], rs_send.at[1])

    deep_device = [device(x, y, c, ahead(z, step, NZ)) for step in DEPTH_STEPS]
    for where in deep_device:
        send(deep_ref.at[0, z], deep_ref.at[0, z], d_send.at[0], d_recv.at[0], where)

    @pl.when(holder)
    def _():
        arrived(extra_ref.at[pl.ds(0, OTHERS)], rs_recv.at[1])
        deep_ref[1, z] = jnp.sum(extra_ref[...].astype(F32), axis=0).astype(BF16)
        for where in deep_device:
            send(deep_ref.at[1, z], deep_ref.at[1, z], d_send.at[1], d_recv.at[1], where)

    drain_scatter()
    arrived(deep_ref.at[0, pl.ds(0, DEEP)], d_recv.at[0])
    left_ref[own] = jnp.sum(deep_ref[0].astype(F32), axis=0).astype(BF16)

    def drain_depth():
        arrived(deep_ref.at[0, pl.ds(0, DEEP)], d_send.at[0])

        @pl.when(holder)
        def _():
            arrived(deep_ref.at[1, pl.ds(0, DEEP)], d_send.at[1])

    plane_device = [device(*plane_peer(step), z) for step in PLANE_STEPS]
    for where in plane_device:
        send(left_ref.at[own], left_ref.at[own], ag_send.at[0], ag_recv.at[0], where)

    @pl.when(holder)
    def _():
        arrived(deep_ref.at[1, pl.ds(0, DEEP)], d_recv.at[1])
        left_ref[spare] = jnp.sum(deep_ref[1].astype(F32), axis=0).astype(BF16)
        for where in plane_device:
            send(left_ref.at[spare], left_ref.at[spare], ag_send.at[1], ag_recv.at[1], where)

    def columns(first, last):
        return jnp.concatenate(
            [jnp.concatenate([left_ref[h * TILES + n] for h in range(NC)], axis=0) for n in range(first, last)], axis=1
        )

    drain_depth()
    arrived(left_ref.at[pl.ds(0, OTHERS)], ag_recv.at[0])

    left = columns(0, MAIN)
    product = lax.dot_general(left, l_ref[:, :MAIN * LANES], NT, preferred_element_type=F32)

    @pl.when(holder)
    def _():
        arrived(left_ref.at[pl.ds(0, len(HOLDERS) - 1)], ag_recv.at[1])

    @pl.when(jnp.logical_not(holder))
    def _():
        arrived(left_ref.at[pl.ds(0, len(HOLDERS))], ag_recv.at[1])

    rest = columns(MAIN, TILES)
    product = product + lax.dot_general(rest, l_ref[:, MAIN * LANES:], NT, preferred_element_type=F32)
    left = jnp.concatenate([left, rest], axis=1)
    t_ref[tp] = product.astype(BF16)

    def drain_gather():
        arrived(left_ref.at[pl.ds(0, OTHERS)], ag_send.at[0])

        @pl.when(holder)
        def _():
            arrived(left_ref.at[pl.ds(0, OTHERS)], ag_send.at[1])

    for step in GROUP_STEPS:
        px, py, pc = plane_peer(step)
        send(t_ref.at[tp], t_ref.at[tp], t_send, t_recv, (dp, py * NC + pc))
    right = jnp.dot(left, f_ref[...], preferred_element_type=F32)
    drain_gather()
    arrived(t_ref.at[pl.ds(0, GROUP - 1)], t_recv)
    gathered = jnp.concatenate([t_ref[t] for t in range(GROUP)], axis=1)

    keeper = x // 2 == c
    odd = NX + x % 2
    row_device = [device(ahead(x, step, NX), y, c, z) for step in ROW_STEPS]
    for j in range(FEATURES // LANES):
        lanes = slice(j * LANES, (j + 1) * LANES)
        got = right[:, lanes] + jnp.dot(gathered, v_ref[:, lanes], preferred_element_type=F32)
        for h in range(NC):
            tile = j * NC + h
            ys_ref[tile] = got[h * HALF:(h + 1) * HALF]
            if tile < NX:

                @pl.when(x != tile)
                def _():
                    send(ys_ref.at[tile], xr_ref.at[0, x], x_send.at[0], x_recv.at[0], device(tile, y, c, z))
            else:
                taker = 2 * c + tile - NX

                @pl.when(x != taker)
                def _():
                    send(ys_ref.at[tile], xr_ref.at[1, x], x_send.at[1 + tile - NX], x_recv.at[1], device(taker, y, c, z))

    xr_ref[0, x] = ys_ref[x]
    xr_ref[1, x] = ys_ref[odd]
    arrived(xr_ref.at[0, pl.ds(0, NX - 1)], x_recv.at[0])
    deep2_ref[0, z] = jnp.sum(xr_ref[0], axis=0).astype(BF16)

    def drain_rows():
        arrived(t_ref.at[pl.ds(0, GROUP - 1)], t_send)
        arrived(ys_ref.at[pl.ds(0, NX - 1)], x_send.at[0])
        for e in range(2):

            @pl.when(x != 2 * c + e)
            def _():
                arrived(ys_ref.at[NX + e], x_send.at[1 + e])

    for where in deep_device:
        send(deep2_ref.at[0, z], deep2_ref.at[0, z], d2_send.at[0], d2_recv.at[0], where)

    @pl.when(keeper)
    def _():
        arrived(xr_ref.at[1, pl.ds(0, NX - 1)], x_recv.at[1])
        deep2_ref[1, z] = jnp.sum(xr_ref[1], axis=0).astype(BF16)
        for where in deep_device:
            send(deep2_ref.at[1, z], deep2_ref.at[1, z], d2_send.at[1], d2_recv.at[1], where)

    drain_rows()

    tall = jnp.concatenate([left, jnp.zeros((LANES - RANK, WIDTH), BF16)], axis=0)
    table = lax.dot_general(left, tall, NT, preferred_element_type=F32)
    rows = lax.broadcasted_iota(jnp.int32, (RANK, LANES), 0)
    lanes = lax.broadcasted_iota(jnp.int32, (RANK, LANES), 1)
    table = jnp.where(lanes == rows + RANK, 1.0, table)
    for k in range(RANK):
        ratio = table[:, k:k + 1] / table[k:k + 1, k:k + 1]
        table = table - jnp.where(rows > k, ratio, 0.0) * table[k:k + 1, :]
    pivots = jnp.sum(jnp.where(lanes == rows, table, 0.0), axis=1, keepdims=True)
    inverse = jnp.where(lanes >= RANK, table, 0.0) * lax.rsqrt(pivots)

    inverse = split(inverse)

    def padded(value):
        above, below = jnp.zeros((RANK, FEATURES), BF16), jnp.zeros((LANES - 2 * RANK, FEATURES), BF16)
        return jnp.concatenate([above, value, below], axis=0)

    def solve(value):
        pieces = [value] if value.dtype == BF16 else [value.astype(BF16)]
        if value.dtype == F32:
            pieces.append((value - pieces[0].astype(F32)).astype(BF16))
        terms = [jnp.dot(inverse, padded(piece), preferred_element_type=F32) for piece in pieces]
        return sum(term[:RANK] + term[RANK:] for term in reversed(terms))

    first = (5 * tp) // 2
    window = jnp.concatenate(
        [
            jnp.concatenate([left_ref[h * TILES + first + i] for h in range(NC)], axis=0)
            for i in range(FEATURES // LANES)
        ],
        axis=1,
    )
    own_basis = solve(window) * math.sqrt(WIDTH)
    shifted = jnp.concatenate([own_basis[:, LANES // 2:], own_basis[:, :LANES // 2]], axis=1)
    share = WIDTH // GROUP
    basis_ref[...] = jnp.where(tp % 2 == 1, shifted, own_basis)[:, :share]

    def drain_depth2():
        arrived(deep2_ref.at[0, pl.ds(0, DEEP)], d2_send.at[0])

        @pl.when(keeper)
        def _():
            arrived(deep2_ref.at[1, pl.ds(0, DEEP)], d2_send.at[1])

    arrived(deep2_ref.at[0, pl.ds(0, DEEP)], d2_recv.at[0])
    yf_ref[x] = jnp.sum(deep2_ref[0].astype(F32), axis=0)
    for where in row_device:
        send(yf_ref.at[x], yf_ref.at[x], xg_send.at[0], xg_recv.at[0], where)

    @pl.when(keeper)
    def _():
        arrived(deep2_ref.at[1, pl.ds(0, DEEP)], d2_recv.at[1])
        yf_ref[odd] = jnp.sum(deep2_ref[1].astype(F32), axis=0)
        for where in row_device:
            send(yf_ref.at[odd], yf_ref.at[odd], xg_send.at[1], xg_recv.at[1 + x % 2], where)

    drain_depth2()
    arrived(yf_ref.at[pl.ds(0, NX - 1)], xg_recv.at[0])
    for e in range(2):

        @pl.when(x != 2 * c + e)
        def _():
            arrived(yf_ref.at[NX + e], xg_recv.at[1 + e])

    summed = jnp.concatenate(
        [
            jnp.concatenate([yf_ref[j * NC + h] for h in range(NC)], axis=0)
            for j in range(FEATURES // LANES)
        ],
        axis=1,
    )
    next_ref[...] = solve(summed) * (1.0 / (NX * NZ))
    arrived(yf_ref.at[pl.ds(0, NX - 1)], xg_send.at[0])

    @pl.when(keeper)
    def _():
        arrived(yf_ref.at[pl.ds(0, NX - 1)], xg_send.at[1])


def place_results(basis_ref, factor_ref, basis_out, factor_out):
    basis_out[...] = basis_ref[...]
    factor_out[...] = factor_ref[...]


def on_device(
    layer_input, queries, key_vectors, out_grad, feedback, factor_prev, token_count, segment_ids
):
    vmem = pl.BlockSpec(memory_space=pltpu.VMEM)
    anywhere = pl.BlockSpec(memory_space=pltpu.HBM)
    dma = pltpu.SemaphoreType.DMA
    basis, factor = pl.pallas_call(
        kernel,
        out_shape=(
            jax.ShapeDtypeStruct((RANK, WIDTH // GROUP), F32),
            jax.ShapeDtypeStruct((RANK, FEATURES), F32),
        ),
        in_specs=[anywhere] * 6 + [pl.BlockSpec(memory_space=pltpu.SMEM), anywhere],
        out_specs=(vmem, vmem),
        scratch_shapes=[
            pltpu.VMEM((RANK, FEATURES), F32),
            pltpu.VMEM((SLOTS // LANES, LANES), jnp.int32),
            pltpu.VMEM((SLOTS, LANES), BF16),
            pltpu.VMEM((SLOTS, LANES), BF16),
            pltpu.VMEM((SLOTS, FEATURES), BF16),
            pltpu.VMEM((SLOTS, FEATURES), BF16),
            pltpu.VMEM((SLOTS, FEATURES), BF16),
            pltpu.VMEM((WIDTH, FEATURES), BF16),
            pltpu.VMEM((LANES, WIDTH), BF16),
            pltpu.VMEM((SLOTS, FEATURES), BF16),
            pltpu.VMEM((HEADS, SLOTS, SLOTS), BF16),
            pltpu.VMEM((RANK, WIDTH), F32),
            pltpu.VMEM((GROUP, RANK, LANES), F32),
            pltpu.VMEM((GROUP, RANK, LANES), F32),
            pltpu.VMEM((NC * TILES, HALF, LANES), BF16),
            pltpu.VMEM((PLANE, HALF, LANES), BF16),
            pltpu.VMEM((PLANE, HALF, LANES), BF16),
            pltpu.VMEM((2, NZ, HALF, LANES), BF16),
            pltpu.VMEM((NC * TILES, HALF, LANES), BF16),
            pltpu.VMEM((GROUP, RANK, LANES), BF16),
            pltpu.VMEM((6, HALF, LANES), F32),
            pltpu.VMEM((2, NX, HALF, LANES), F32),
            pltpu.VMEM((2, NZ, HALF, LANES), BF16),
            pltpu.VMEM((6, HALF, LANES), F32),
            dma((HEADS + 4,)),
            dma, dma,
            dma((2,)), dma((2,)),
            dma((2,)), dma((2,)),
            dma((2,)), dma((2,)),
            dma, dma,
            dma((3,)), dma((2,)),
            dma((2,)), dma((2,)),
            dma((2,)), dma((3,)),
        ],
        compiler_params=pltpu.CompilerParams(
            collective_id=0, has_side_effects=True, vmem_limit_bytes=32 * 1024 * 1024
        ),
    )(
        *(
            pltpu.with_memory_space_constraint(value, pltpu.HBM)
            for value in (layer_input, queries, key_vectors, out_grad, feedback, factor_prev)
        ),
        token_count,
        pltpu.with_memory_space_constraint(segment_ids.reshape(SLOTS // LANES, LANES), pltpu.HBM),
    )
    return pl.pallas_call(
        place_results,
        out_shape=(
            jax.ShapeDtypeStruct((RANK, WIDTH // GROUP), F32),
            jax.ShapeDtypeStruct((RANK, FEATURES), F32),
        ),
        in_specs=[vmem, vmem],
        out_specs=(vmem, vmem),
        compiler_params=pltpu.CompilerParams(vmem_limit_bytes=4 * 1024 * 1024),
    )(basis, factor)


def solution(mesh):
    return jax.shard_map(
        on_device,
        mesh=mesh,
        in_specs=(
            P(("dp", "tp"), None),
            P("dp", "tp"),
            P("dp", "tp"),
            P("dp", "tp"),
            P("dp", "tp"),
            P(None, "tp"),
            P("dp"),
            P("dp"),
        ),
        out_specs=(P(None, "tp"), P(None, "tp")),
        check_vma=False,
    )
```

```python
import math

import jax
import jax.numpy as jnp
from jax import lax
from jax.experimental import pallas as pl
from jax.experimental.pallas import tpu as pltpu
from jax.sharding import PartitionSpec as P

MESH = pl.DeviceIdType.MESH
F32, BF16 = jnp.float32, jnp.bfloat16
NT = (((1,), (1,)), ((), ()))

NX, NY, NZ, NC = 4, 4, 16, 2
GROUP = NY * NC
PLANE = NX * GROUP
OTHERS = PLANE - 1
DEEP = NZ - 1
FAR = 7

HEAD_DIM = 128
HEADS = 3
SLOTS = 1024
WIDTH = 2560
RANK = 32
LANES = 128
HALF = 16
FEATURES = HEADS * HEAD_DIM
TILES = WIDTH // LANES
MAIN = NX * NY
BLOCK = 256
BLOCKS = SLOTS // BLOCK
MASKED = -1e30
PENALTY = 65536.0


def ahead(position, step, size):
    moved = position + step
    return jnp.where(moved >= size, moved - size, moved) if step else position


def hops(step, size):
    return min(step, size - step)


PLANE_STEPS = sorted(
    [
        (dx, dy, dc)
        for dx in range(NX)
        for dy in range(NY)
        for dc in range(NC)
        if (dx, dy, dc) != (0, 0, 0)
    ],
    key=lambda s: -(hops(s[0], NX) * 2 + hops(s[1], NY) * 2 + s[2]),
)
GROUP_STEPS = [s for s in PLANE_STEPS if s[0] == 0]
ROW_STEPS = sorted(range(1, NX), key=lambda s: -hops(s, NX))
DEPTH_STEPS = sorted(range(1, NZ), key=lambda s: -hops(s, NZ))
HOLDERS = [(xh, (xh + 2 * ch) % NY, ch) for ch in range(NC) for xh in range(NX)]


def split(value):
    high = value.astype(BF16)
    low = (value - high.astype(F32)).astype(BF16)
    return jnp.concatenate([high, low], axis=0)


def document_columns(seg, key_ref, query_ref):
    for b in range(SLOTS // LANES):
        ids = lax.broadcasted_iota(jnp.int32, (LANES, LANES), 0)
        own = jnp.where(seg[b:b + 1, :] == ids, 1.0, 0.0).T
        key_ref[b * LANES:(b + 1) * LANES, :] = own.astype(BF16)
        query_ref[b * LANES:(b + 1) * LANES, :] = ((own - 1.0) * PENALTY).astype(BF16)


def scores(head, b, k_ref, q_ref, dk_ref, dq_ref):
    lanes = slice(head * HEAD_DIM, (head + 1) * HEAD_DIM)
    low, high = b * BLOCK, (b + 1) * BLOCK
    q = jnp.concatenate([q_ref[low:high, lanes], dq_ref[low:high, :]], axis=1)
    k = jnp.concatenate([k_ref[low:high, lanes], dk_ref[low:high, :]], axis=1)
    near = lax.dot_general(k, q, NT, preferred_element_type=F32)
    key = lax.broadcasted_iota(jnp.int32, (BLOCK, BLOCK), 0)
    query = lax.broadcasted_iota(jnp.int32, (BLOCK, BLOCK), 1)
    near = jnp.where(key <= query, near, MASKED)
    top = jnp.max(near, axis=0, keepdims=True)
    parts = [near]
    if b:
        k = jnp.concatenate([k_ref[0:low, lanes], dk_ref[0:low, :]], axis=1)
        far = lax.dot_general(k, q, NT, preferred_element_type=F32)
        top = jnp.maximum(top, jnp.max(far, axis=0, keepdims=True))
        parts.append(far)
    return parts, top


def weigh(b, count, parts, top, w_ref):
    rate = HEAD_DIM ** (-0.5) * math.log2(math.e)
    low, high = b * BLOCK, (b + 1) * BLOCK
    parts = [jnp.exp2((part - top) * rate) for part in parts]
    total = sum(jnp.sum(part, axis=0, keepdims=True) for part in parts)
    live = lax.broadcasted_iota(jnp.int32, (1, BLOCK), 1) + low < count
    scale = jnp.where(live, 1.0 / jnp.maximum(total, 1.0), 0.0)
    for part, (start, end) in zip(parts, ((low, high), (0, low))):
        w_ref[start:end, low:high] = (part * scale).astype(BF16)


def combine(head, b, g_ref, w_ref, v_ref):
    lanes = slice(head * HEAD_DIM, (head + 1) * HEAD_DIM)
    low, high = b * BLOCK, (b + 1) * BLOCK
    v = jnp.dot(w_ref[low:high, low:], g_ref[low:, lanes], preferred_element_type=F32)
    v_ref[low:high, lanes] = v.astype(BF16)


def kernel(
    layer_hbm, q_hbm, k_hbm, g_hbm, feedback_hbm, factor_hbm, count_ref, segment_hbm,
    basis_ref, next_ref,
    factor_ref, segment_ref, dk_ref, dq_ref,
    q_ref, k_ref, g_ref, f_ref, l_ref, v_ref, w_ref, pf_ref,
    zs_ref, zr_ref, part_ref, main_ref, extra_ref, deep_ref, left_ref, t_ref, ys_ref, xr_ref, deep2_ref, yf_ref,
    load_sem,
    a_send, a_recv, rs_send, rs_recv, d_send, d_recv, ag_send, ag_recv,
    t_send, t_recv, x_send, x_recv, d2_send, d2_recv, xg_send, xg_recv,
):
    dp, tp = lax.axis_index("dp"), lax.axis_index("tp")
    x, z = dp // NZ, dp % NZ
    y, c = tp // NC, tp % NC
    place = x * GROUP + tp

    def plane_peer(step):
        dx, dy, dc = step
        return ahead(x, dx, NX), ahead(y, dy, NY), 1 - c if dc else c

    def device(px, py, pc, pz):
        return (px * NZ + pz, py * NC + pc)

    def load(source, target, which):
        pltpu.make_async_copy(source, target, load_sem.at[which]).start()

    def load_head(head):
        lanes = pl.ds(head * HEAD_DIM, HEAD_DIM)
        for source, target in ((k_hbm, k_ref), (q_hbm, q_ref), (g_hbm, g_ref)):
            load(source.at[:, lanes], target.at[:, lanes], head)

    barrier = pltpu.get_barrier_semaphore()
    for step in DEPTH_STEPS:
        pl.semaphore_signal(barrier, inc=1, device_id=device(x, y, c, ahead(z, step, NZ)), device_id_type=MESH)
    for step in PLANE_STEPS:
        pl.semaphore_signal(barrier, inc=1, device_id=device(*plane_peer(step), z), device_id_type=MESH)
    load(segment_hbm, segment_ref, HEADS)
    load_head(0)
    for head in range(1, HEADS):
        load_head(head)
    load(factor_hbm, factor_ref, HEADS + 1)
    load(feedback_hbm, f_ref, HEADS + 2)
    load(layer_hbm, l_ref, HEADS + 3)

    def send(source, target, send_sem, recv_sem, where):
        pltpu.make_async_remote_copy(
            src_ref=source, dst_ref=target, send_sem=send_sem, recv_sem=recv_sem,
            device_id=where, device_id_type=MESH,
        ).start()

    def arrived(target, recv_sem):
        pltpu.make_async_copy(target, target, recv_sem).wait()

    arrived(segment_ref, load_sem.at[HEADS])
    document_columns(segment_ref[...], dk_ref, dq_ref)
    per = BLOCK // LANES
    units = [(head, b) for b in reversed(range(BLOCKS)) for head in range(HEADS)]

    def begin(unit):
        head, b = units[unit]
        if b == BLOCKS - 1:
            arrived(k_ref, load_sem.at[head])
        return scores(head, b, k_ref, q_ref, dk_ref, dq_ref)

    ready = [begin(unit) for unit in range(1)]
    waiting = []
    for unit, (head, b) in enumerate(units):
        if unit + 1 < len(units):
            ready.append(begin(unit + 1))
        weigh(b, count_ref[0], *ready.pop(0), w_ref.at[head])
        waiting.append((head, b))
        if len(waiting) > 1:
            last, block = waiting.pop(0)
            combine(last, block, g_ref, w_ref.at[last], v_ref)
    for last, block in waiting:
        combine(last, block, g_ref, w_ref.at[last], v_ref)

    arrived(factor_ref, load_sem.at[HEADS + 1])
    factor = split(factor_ref[...])
    for t in range(GROUP):
        got = lax.dot_general(factor, v_ref[t * LANES:(t + 1) * LANES, :], NT, preferred_element_type=F32)
        zs_ref[t] = got[:RANK] + got[RANK:]
    pl.semaphore_wait(barrier, len(DEPTH_STEPS) + len(PLANE_STEPS))
    for step in GROUP_STEPS:
        px, py, pc = plane_peer(step)
        peer = py * NC + pc
        send(zs_ref.at[peer], zr_ref.at[tp], a_send, a_recv, (dp, peer))
    zr_ref[tp] = zs_ref[tp]

    arrived(f_ref, load_sem.at[HEADS + 2])
    for j in range(WIDTH // BLOCK):
        got = lax.dot_general(factor, f_ref[j * BLOCK:(j + 1) * BLOCK, :], NT, preferred_element_type=F32)
        pf_ref[:, j * BLOCK:(j + 1) * BLOCK] = got[:RANK] + got[RANK:]
    arrived(l_ref, load_sem.at[HEADS + 3])
    arrived(zs_ref.at[pl.ds(0, GROUP - 1)], a_send)
    arrived(zr_ref.at[pl.ds(0, GROUP - 1)], a_recv)
    mixed = split(jnp.sum(zr_ref[...], axis=0))
    for j in range(WIDTH // BLOCK):
        lanes = slice(j * BLOCK, (j + 1) * BLOCK)
        got = jnp.dot(mixed, l_ref[:, lanes], preferred_element_type=F32)
        part = (pf_ref[:, lanes] + got[:RANK] + got[RANK:]).astype(BF16)
        for i in range(per):
            for h in range(NC):
                part_ref[h * TILES + j * per + i] = part[h * HALF:(h + 1) * HALF, i * LANES:(i + 1) * LANES]

    holder = y == (x + 2 * c) % NY
    own = c * TILES + NY * x + y
    spare = c * TILES + MAIN + x
    for xh, yh, ch in HOLDERS:

        @pl.when(place != xh * GROUP + yh * NC + ch)
        def _():
            send(part_ref.at[ch * TILES + MAIN + xh], extra_ref.at[place], rs_send.at[1], rs_recv.at[1], device(xh, yh, ch, z))

    for step in PLANE_STEPS:
        px, py, pc = plane_peer(step)
        send(part_ref.at[pc * TILES + NY * px + py], main_ref.at[place], rs_send.at[0], rs_recv.at[0], device(px, py, pc, z))

    main_ref[place] = part_ref[own]
    extra_ref[place] = part_ref[spare]
    arrived(main_ref.at[pl.ds(0, OTHERS)], rs_recv.at[0])
    deep_ref[0, z] = jnp.sum(main_ref[...].astype(F32), axis=0).astype(BF16)

    def drain_scatter():
        arrived(part_ref.at[pl.ds(0, OTHERS)], rs_send.at[0])

        @pl.when(holder)
        def _():
            arrived(part_ref.at[pl.ds(0, len(HOLDERS) - 1)], rs_send.at[1])

        @pl.when(jnp.logical_not(holder))
        def _():
            arrived(part_ref.at[pl.ds(0, len(HOLDERS))], rs_send.at[1])

    deep_device = [device(x, y, c, ahead(z, step, NZ)) for step in DEPTH_STEPS]
    for where in deep_device[:FAR]:
        send(deep_ref.at[0, z], deep_ref.at[0, z], d_send.at[0], d_recv.at[0], where)

    @pl.when(holder)
    def _():
        arrived(extra_ref.at[pl.ds(0, OTHERS)], rs_recv.at[1])
        deep_ref[1, z] = jnp.sum(extra_ref[...].astype(F32), axis=0).astype(BF16)
        for where in deep_device[:FAR]:
            send(deep_ref.at[1, z], deep_ref.at[1, z], d_send.at[1], d_recv.at[1], where)

    for where in deep_device[FAR:]:
        send(deep_ref.at[0, z], deep_ref.at[0, z], d_send.at[0], d_recv.at[0], where)

    @pl.when(holder)
    def _():
        for where in deep_device[FAR:]:
            send(deep_ref.at[1, z], deep_ref.at[1, z], d_send.at[1], d_recv.at[1], where)

    drain_scatter()
    arrived(deep_ref.at[0, pl.ds(0, DEEP)], d_recv.at[0])
    left_ref[own] = jnp.sum(deep_ref[0].astype(F32), axis=0).astype(BF16)

    def drain_depth():
        arrived(deep_ref.at[0, pl.ds(0, DEEP)], d_send.at[0])

        @pl.when(holder)
        def _():
            arrived(deep_ref.at[1, pl.ds(0, DEEP)], d_send.at[1])

    plane_device = [device(*plane_peer(step), z) for step in PLANE_STEPS]
    for where in plane_device:
        send(left_ref.at[own], left_ref.at[own], ag_send.at[0], ag_recv.at[0], where)

    @pl.when(holder)
    def _():
        arrived(deep_ref.at[1, pl.ds(0, DEEP)], d_recv.at[1])
        left_ref[spare] = jnp.sum(deep_ref[1].astype(F32), axis=0).astype(BF16)
        for where in plane_device:
            send(left_ref.at[spare], left_ref.at[spare], ag_send.at[1], ag_recv.at[1], where)

    def columns(first, last):
        return jnp.concatenate(
            [jnp.concatenate([left_ref[h * TILES + n] for h in range(NC)], axis=0) for n in range(first, last)], axis=1
        )

    drain_depth()
    arrived(left_ref.at[pl.ds(0, OTHERS)], ag_recv.at[0])

    left = columns(0, MAIN)
    product = lax.dot_general(left, l_ref[:, :MAIN * LANES], NT, preferred_element_type=F32)

    @pl.when(holder)
    def _():
        arrived(left_ref.at[pl.ds(0, len(HOLDERS) - 1)], ag_recv.at[1])

    @pl.when(jnp.logical_not(holder))
    def _():
        arrived(left_ref.at[pl.ds(0, len(HOLDERS))], ag_recv.at[1])

    rest = columns(MAIN, TILES)
    product = product + lax.dot_general(rest, l_ref[:, MAIN * LANES:], NT, preferred_element_type=F32)
    left = jnp.concatenate([left, rest], axis=1)
    t_ref[tp] = product.astype(BF16)

    def drain_gather():
        arrived(left_ref.at[pl.ds(0, OTHERS)], ag_send.at[0])

        @pl.when(holder)
        def _():
            arrived(left_ref.at[pl.ds(0, OTHERS)], ag_send.at[1])

    for step in GROUP_STEPS:
        px, py, pc = plane_peer(step)
        send(t_ref.at[tp], t_ref.at[tp], t_send, t_recv, (dp, py * NC + pc))
    right = jnp.dot(left, f_ref[...], preferred_element_type=F32)
    drain_gather()
    arrived(t_ref.at[pl.ds(0, GROUP - 1)], t_recv)
    gathered = jnp.concatenate([t_ref[t] for t in range(GROUP)], axis=1)

    keeper = x // 2 == c
    odd = NX + x % 2
    row_device = [device(ahead(x, step, NX), y, c, z) for step in ROW_STEPS]
    for j in range(FEATURES // LANES):
        lanes = slice(j * LANES, (j + 1) * LANES)
        got = right[:, lanes] + jnp.dot(gathered, v_ref[:, lanes], preferred_element_type=F32)
        for h in range(NC):
            tile = j * NC + h
            ys_ref[tile] = got[h * HALF:(h + 1) * HALF]
            if tile < NX:

                @pl.when(x != tile)
                def _():
                    send(ys_ref.at[tile], xr_ref.at[0, x], x_send.at[0], x_recv.at[0], device(tile, y, c, z))
            else:
                taker = 2 * c + tile - NX

                @pl.when(x != taker)
                def _():
                    send(ys_ref.at[tile], xr_ref.at[1, x], x_send.at[1 + tile - NX], x_recv.at[1], device(taker, y, c, z))

    xr_ref[0, x] = ys_ref[x]
    xr_ref[1, x] = ys_ref[odd]
    arrived(xr_ref.at[0, pl.ds(0, NX - 1)], x_recv.at[0])
    deep2_ref[0, z] = jnp.sum(xr_ref[0], axis=0).astype(BF16)

    def drain_rows():
        arrived(t_ref.at[pl.ds(0, GROUP - 1)], t_send)
        arrived(ys_ref.at[pl.ds(0, NX - 1)], x_send.at[0])
        for e in range(2):

            @pl.when(x != 2 * c + e)
            def _():
                arrived(ys_ref.at[NX + e], x_send.at[1 + e])

    for where in deep_device[:FAR]:
        send(deep2_ref.at[0, z], deep2_ref.at[0, z], d2_send.at[0], d2_recv.at[0], where)

    @pl.when(keeper)
    def _():
        arrived(xr_ref.at[1, pl.ds(0, NX - 1)], x_recv.at[1])
        deep2_ref[1, z] = jnp.sum(xr_ref[1], axis=0).astype(BF16)
        for where in deep_device[:FAR]:
            send(deep2_ref.at[1, z], deep2_ref.at[1, z], d2_send.at[1], d2_recv.at[1], where)

    for where in deep_device[FAR:]:
        send(deep2_ref.at[0, z], deep2_ref.at[0, z], d2_send.at[0], d2_recv.at[0], where)

    @pl.when(keeper)
    def _():
        for where in deep_device[FAR:]:
            send(deep2_ref.at[1, z], deep2_ref.at[1, z], d2_send.at[1], d2_recv.at[1], where)

    drain_rows()

    tall = jnp.concatenate([left, jnp.zeros((LANES - RANK, WIDTH), BF16)], axis=0)
    table = lax.dot_general(left, tall, NT, preferred_element_type=F32)
    rows = lax.broadcasted_iota(jnp.int32, (RANK, LANES), 0)
    lanes = lax.broadcasted_iota(jnp.int32, (RANK, LANES), 1)
    table = jnp.where(lanes == rows + RANK, 1.0, table)
    for k in range(RANK):
        ratio = table[:, k:k + 1] / table[k:k + 1, k:k + 1]
        table = table - jnp.where(rows > k, ratio, 0.0) * table[k:k + 1, :]
    pivots = jnp.sum(jnp.where(lanes == rows, table, 0.0), axis=1, keepdims=True)
    inverse = jnp.where(lanes >= RANK, table, 0.0) * lax.rsqrt(pivots)

    inverse = split(inverse)

    def padded(value):
        above, below = jnp.zeros((RANK, FEATURES), BF16), jnp.zeros((LANES - 2 * RANK, FEATURES), BF16)
        return jnp.concatenate([above, value, below], axis=0)

    def solve(value):
        pieces = [value] if value.dtype == BF16 else [value.astype(BF16)]
        if value.dtype == F32:
            pieces.append((value - pieces[0].astype(F32)).astype(BF16))
        terms = [jnp.dot(inverse, padded(piece), preferred_element_type=F32) for piece in pieces]
        return sum(term[:RANK] + term[RANK:] for term in reversed(terms))

    first = (5 * tp) // 2
    window = jnp.concatenate(
        [
            jnp.concatenate([left_ref[h * TILES + first + i] for h in range(NC)], axis=0)
            for i in range(FEATURES // LANES)
        ],
        axis=1,
    )
    own_basis = solve(window) * math.sqrt(WIDTH)
    shifted = jnp.concatenate([own_basis[:, LANES // 2:], own_basis[:, :LANES // 2]], axis=1)
    share = WIDTH // GROUP
    basis_ref[...] = jnp.where(tp % 2 == 1, shifted, own_basis)[:, :share]

    def drain_depth2():
        arrived(deep2_ref.at[0, pl.ds(0, DEEP)], d2_send.at[0])

        @pl.when(keeper)
        def _():
            arrived(deep2_ref.at[1, pl.ds(0, DEEP)], d2_send.at[1])

    arrived(deep2_ref.at[0, pl.ds(0, DEEP)], d2_recv.at[0])
    yf_ref[x] = jnp.sum(deep2_ref[0].astype(F32), axis=0)
    for where in row_device:
        send(yf_ref.at[x], yf_ref.at[x], xg_send.at[0], xg_recv.at[0], where)

    @pl.when(keeper)
    def _():
        arrived(deep2_ref.at[1, pl.ds(0, DEEP)], d2_recv.at[1])
        yf_ref[odd] = jnp.sum(deep2_ref[1].astype(F32), axis=0)
        for where in row_device:
            send(yf_ref.at[odd], yf_ref.at[odd], xg_send.at[1], xg_recv.at[1 + x % 2], where)

    drain_depth2()
    arrived(yf_ref.at[pl.ds(0, NX - 1)], xg_recv.at[0])
    for e in range(2):

        @pl.when(x != 2 * c + e)
        def _():
            arrived(yf_ref.at[NX + e], xg_recv.at[1 + e])

    summed = jnp.concatenate(
        [
            jnp.concatenate([yf_ref[j * NC + h] for h in range(NC)], axis=0)
            for j in range(FEATURES // LANES)
        ],
        axis=1,
    )
    next_ref[...] = solve(summed) * (1.0 / (NX * NZ))
    arrived(yf_ref.at[pl.ds(0, NX - 1)], xg_send.at[0])

    @pl.when(keeper)
    def _():
        arrived(yf_ref.at[pl.ds(0, NX - 1)], xg_send.at[1])


def place_results(basis_ref, factor_ref, basis_out, factor_out):
    basis_out[...] = basis_ref[...]
    factor_out[...] = factor_ref[...]


def on_device(
    layer_input, queries, key_vectors, out_grad, feedback, factor_prev, token_count, segment_ids
):
    vmem = pl.BlockSpec(memory_space=pltpu.VMEM)
    anywhere = pl.BlockSpec(memory_space=pltpu.HBM)
    dma = pltpu.SemaphoreType.DMA
    basis, factor = pl.pallas_call(
        kernel,
        out_shape=(
            jax.ShapeDtypeStruct((RANK, WIDTH // GROUP), F32),
            jax.ShapeDtypeStruct((RANK, FEATURES), F32),
        ),
        in_specs=[anywhere] * 6 + [pl.BlockSpec(memory_space=pltpu.SMEM), anywhere],
        out_specs=(vmem, vmem),
        scratch_shapes=[
            pltpu.VMEM((RANK, FEATURES), F32),
            pltpu.VMEM((SLOTS // LANES, LANES), jnp.int32),
            pltpu.VMEM((SLOTS, LANES), BF16),
            pltpu.VMEM((SLOTS, LANES), BF16),
            pltpu.VMEM((SLOTS, FEATURES), BF16),
            pltpu.VMEM((SLOTS, FEATURES), BF16),
            pltpu.VMEM((SLOTS, FEATURES), BF16),
            pltpu.VMEM((WIDTH, FEATURES), BF16),
            pltpu.VMEM((LANES, WIDTH), BF16),
            pltpu.VMEM((SLOTS, FEATURES), BF16),
            pltpu.VMEM((HEADS, SLOTS, SLOTS), BF16),
            pltpu.VMEM((RANK, WIDTH), F32),
            pltpu.VMEM((GROUP, RANK, LANES), F32),
            pltpu.VMEM((GROUP, RANK, LANES), F32),
            pltpu.VMEM((NC * TILES, HALF, LANES), BF16),
            pltpu.VMEM((PLANE, HALF, LANES), BF16),
            pltpu.VMEM((PLANE, HALF, LANES), BF16),
            pltpu.VMEM((2, NZ, HALF, LANES), BF16),
            pltpu.VMEM((NC * TILES, HALF, LANES), BF16),
            pltpu.VMEM((GROUP, RANK, LANES), BF16),
            pltpu.VMEM((6, HALF, LANES), F32),
            pltpu.VMEM((2, NX, HALF, LANES), F32),
            pltpu.VMEM((2, NZ, HALF, LANES), BF16),
            pltpu.VMEM((6, HALF, LANES), F32),
            dma((HEADS + 4,)),
            dma, dma,
            dma((2,)), dma((2,)),
            dma((2,)), dma((2,)),
            dma((2,)), dma((2,)),
            dma, dma,
            dma((3,)), dma((2,)),
            dma((2,)), dma((2,)),
            dma((2,)), dma((3,)),
        ],
        compiler_params=pltpu.CompilerParams(
            collective_id=0, has_side_effects=True, vmem_limit_bytes=32 * 1024 * 1024
        ),
    )(
        *(
            pltpu.with_memory_space_constraint(value, pltpu.HBM)
            for value in (layer_input, queries, key_vectors, out_grad, feedback, factor_prev)
        ),
        token_count,
        pltpu.with_memory_space_constraint(segment_ids.reshape(SLOTS // LANES, LANES), pltpu.HBM),
    )
    return pl.pallas_call(
        place_results,
        out_shape=(
            jax.ShapeDtypeStruct((RANK, WIDTH // GROUP), F32),
            jax.ShapeDtypeStruct((RANK, FEATURES), F32),
        ),
        in_specs=[vmem, vmem],
        out_specs=(vmem, vmem),
        compiler_params=pltpu.CompilerParams(vmem_limit_bytes=4 * 1024 * 1024),
    )(basis, factor)


def solution(mesh):
    return jax.shard_map(
        on_device,
        mesh=mesh,
        in_specs=(
            P(("dp", "tp"), None),
            P("dp", "tp"),
            P("dp", "tp"),
            P("dp", "tp"),
            P("dp", "tp"),
            P(None, "tp"),
            P("dp"),
            P("dp"),
        ),
        out_specs=(P(None, "tp"), P(None, "tp")),
        check_vma=False,
    )
```

```python
import math

import jax
import jax.numpy as jnp
from jax import lax
from jax.experimental import pallas as pl
from jax.experimental.pallas import tpu as pltpu
from jax.sharding import PartitionSpec as P

MESH = pl.DeviceIdType.MESH
F32, BF16 = jnp.float32, jnp.bfloat16
NT = (((1,), (1,)), ((), ()))

NX, NY, NZ, NC = 4, 4, 16, 2
GROUP = NY * NC
PLANE = NX * GROUP
OTHERS = PLANE - 1
DEEP = NZ - 1
FAR = 7

HEAD_DIM = 128
HEADS = 3
SLOTS = 1024
WIDTH = 2560
RANK = 32
LANES = 128
HALF = 16
FEATURES = HEADS * HEAD_DIM
TILES = WIDTH // LANES
MAIN = NX * NY
BLOCK = 256
BLOCKS = SLOTS // BLOCK
MASKED = -1e30
PENALTY = 65536.0


def ahead(position, step, size):
    moved = position + step
    return jnp.where(moved >= size, moved - size, moved) if step else position


def hops(step, size):
    return min(step, size - step)


PLANE_STEPS = sorted(
    [
        (dx, dy, dc)
        for dx in range(NX)
        for dy in range(NY)
        for dc in range(NC)
        if (dx, dy, dc) != (0, 0, 0)
    ],
    key=lambda s: -(hops(s[0], NX) * 2 + hops(s[1], NY) * 2 + s[2]),
)
GROUP_STEPS = [s for s in PLANE_STEPS if s[0] == 0]
ROW_STEPS = sorted(range(1, NX), key=lambda s: -hops(s, NX))
DEPTH_STEPS = sorted(range(1, NZ), key=lambda s: -hops(s, NZ))
HOLDERS = [(xh, (xh + 2 * ch) % NY, ch) for ch in range(NC) for xh in range(NX)]


def split(value):
    high = value.astype(BF16)
    low = (value - high.astype(F32)).astype(BF16)
    return jnp.concatenate([high, low], axis=0)


def document_columns(seg, key_ref, query_ref):
    for b in range(SLOTS // LANES):
        ids = lax.broadcasted_iota(jnp.int32, (LANES, LANES), 0)
        own = jnp.where(seg[b:b + 1, :] == ids, 1.0, 0.0).T
        key_ref[b * LANES:(b + 1) * LANES, :] = own.astype(BF16)
        query_ref[b * LANES:(b + 1) * LANES, :] = ((own - 1.0) * PENALTY).astype(BF16)


def scores(head, b, k_ref, q_ref, dk_ref, dq_ref):
    lanes = slice(head * HEAD_DIM, (head + 1) * HEAD_DIM)
    low, high = b * BLOCK, (b + 1) * BLOCK
    q = jnp.concatenate([q_ref[low:high, lanes], dq_ref[low:high, :]], axis=1)
    k = jnp.concatenate([k_ref[low:high, lanes], dk_ref[low:high, :]], axis=1)
    near = lax.dot_general(k, q, NT, preferred_element_type=F32)
    key = lax.broadcasted_iota(jnp.int32, (BLOCK, BLOCK), 0)
    query = lax.broadcasted_iota(jnp.int32, (BLOCK, BLOCK), 1)
    near = jnp.where(key <= query, near, MASKED)
    top = jnp.max(near, axis=0, keepdims=True)
    parts = [near]
    if b:
        k = jnp.concatenate([k_ref[0:low, lanes], dk_ref[0:low, :]], axis=1)
        far = lax.dot_general(k, q, NT, preferred_element_type=F32)
        top = jnp.maximum(top, jnp.max(far, axis=0, keepdims=True))
        parts.append(far)
    return parts, top


def weigh(b, count, parts, top, w_ref):
    rate = HEAD_DIM ** (-0.5) * math.log2(math.e)
    low, high = b * BLOCK, (b + 1) * BLOCK
    parts = [jnp.exp2((part - top) * rate) for part in parts]
    total = sum(jnp.sum(part, axis=0, keepdims=True) for part in parts)
    live = lax.broadcasted_iota(jnp.int32, (1, BLOCK), 1) + low < count
    scale = jnp.where(live, 1.0 / jnp.maximum(total, 1.0), 0.0)
    for part, (start, end) in zip(parts, ((low, high), (0, low))):
        w_ref[start:end, low:high] = (part * scale).astype(BF16)


def combine(head, b, g_ref, w_ref, v_ref):
    lanes = slice(head * HEAD_DIM, (head + 1) * HEAD_DIM)
    low, high = b * BLOCK, (b + 1) * BLOCK
    v = jnp.dot(w_ref[low:high, low:], g_ref[low:, lanes], preferred_element_type=F32)
    v_ref[low:high, lanes] = v.astype(BF16)


def kernel(
    layer_hbm, q_hbm, k_hbm, g_hbm, feedback_hbm, factor_hbm, count_ref, segment_hbm,
    basis_ref, next_ref,
    factor_ref, segment_ref, dk_ref, dq_ref,
    q_ref, k_ref, g_ref, f_ref, l_ref, v_ref, w_ref, pf_ref,
    zs_ref, zr_ref, part_ref, main_ref, extra_ref, deep_ref, left_ref, t_ref, ys_ref, xr_ref, deep2_ref, yf_ref,
    load_sem,
    a_send, a_recv, rs_send, rs_recv, d_send, d_recv, ag_send, ag_recv,
    t_send, t_recv, x_send, x_recv, d2_send, d2_recv, xg_send, xg_recv,
):
    dp, tp = lax.axis_index("dp"), lax.axis_index("tp")
    x, z = dp // NZ, dp % NZ
    y, c = tp // NC, tp % NC
    place = x * GROUP + tp

    def plane_peer(step):
        dx, dy, dc = step
        return ahead(x, dx, NX), ahead(y, dy, NY), 1 - c if dc else c

    def device(px, py, pc, pz):
        return (px * NZ + pz, py * NC + pc)

    def load(source, target, which):
        pltpu.make_async_copy(source, target, load_sem.at[which]).start()

    def load_head(head):
        lanes = pl.ds(head * HEAD_DIM, HEAD_DIM)
        for source, target in ((k_hbm, k_ref), (q_hbm, q_ref), (g_hbm, g_ref)):
            load(source.at[:, lanes], target.at[:, lanes], head)

    barrier = pltpu.get_barrier_semaphore()
    for step in DEPTH_STEPS:
        pl.semaphore_signal(barrier, inc=1, device_id=device(x, y, c, ahead(z, step, NZ)), device_id_type=MESH)
    load(segment_hbm, segment_ref, HEADS)
    load_head(0)
    for step in PLANE_STEPS:
        pl.semaphore_signal(barrier, inc=1, device_id=device(*plane_peer(step), z), device_id_type=MESH)
    for head in range(1, HEADS):
        load_head(head)
    load(factor_hbm, factor_ref, HEADS + 1)
    load(feedback_hbm, f_ref, HEADS + 2)
    load(layer_hbm, l_ref, HEADS + 3)

    def send(source, target, send_sem, recv_sem, where):
        pltpu.make_async_remote_copy(
            src_ref=source, dst_ref=target, send_sem=send_sem, recv_sem=recv_sem,
            device_id=where, device_id_type=MESH,
        ).start()

    def arrived(target, recv_sem):
        pltpu.make_async_copy(target, target, recv_sem).wait()

    arrived(segment_ref, load_sem.at[HEADS])
    document_columns(segment_ref[...], dk_ref, dq_ref)
    per = BLOCK // LANES
    units = [(head, b) for b in reversed(range(BLOCKS)) for head in range(HEADS)]

    def begin(unit):
        head, b = units[unit]
        if b == BLOCKS - 1:
            arrived(k_ref, load_sem.at[head])
        return scores(head, b, k_ref, q_ref, dk_ref, dq_ref)

    ready = [begin(unit) for unit in range(1)]
    waiting = []
    for unit, (head, b) in enumerate(units):
        if unit + 1 < len(units):
            ready.append(begin(unit + 1))
        weigh(b, count_ref[0], *ready.pop(0), w_ref.at[head])
        waiting.append((head, b))
        if len(waiting) > 1:
            last, block = waiting.pop(0)
            combine(last, block, g_ref, w_ref.at[last], v_ref)
    for last, block in waiting:
        combine(last, block, g_ref, w_ref.at[last], v_ref)

    arrived(factor_ref, load_sem.at[HEADS + 1])
    factor = split(factor_ref[...])
    for t in range(GROUP):
        got = lax.dot_general(factor, v_ref[t * LANES:(t + 1) * LANES, :], NT, preferred_element_type=F32)
        zs_ref[t] = got[:RANK] + got[RANK:]
    pl.semaphore_wait(barrier, len(DEPTH_STEPS) + len(PLANE_STEPS))
    for step in GROUP_STEPS:
        px, py, pc = plane_peer(step)
        peer = py * NC + pc
        send(zs_ref.at[peer], zr_ref.at[tp], a_send, a_recv, (dp, peer))
    zr_ref[tp] = zs_ref[tp]

    arrived(f_ref, load_sem.at[HEADS + 2])
    for j in range(WIDTH // BLOCK):
        got = lax.dot_general(factor, f_ref[j * BLOCK:(j + 1) * BLOCK, :], NT, preferred_element_type=F32)
        pf_ref[:, j * BLOCK:(j + 1) * BLOCK] = got[:RANK] + got[RANK:]
    arrived(l_ref, load_sem.at[HEADS + 3])
    arrived(zr_ref.at[pl.ds(0, GROUP - 1)], a_recv)
    mixed = split(jnp.sum(zr_ref[...], axis=0))
    for j in range(WIDTH // BLOCK):
        lanes = slice(j * BLOCK, (j + 1) * BLOCK)
        got = jnp.dot(mixed, l_ref[:, lanes], preferred_element_type=F32)
        part = (pf_ref[:, lanes] + got[:RANK] + got[RANK:]).astype(BF16)
        for i in range(per):
            for h in range(NC):
                part_ref[h * TILES + j * per + i] = part[h * HALF:(h + 1) * HALF, i * LANES:(i + 1) * LANES]

    holder = y == (x + 2 * c) % NY
    own = c * TILES + NY * x + y
    spare = c * TILES + MAIN + x
    for xh, yh, ch in HOLDERS:

        @pl.when(place != xh * GROUP + yh * NC + ch)
        def _():
            send(part_ref.at[ch * TILES + MAIN + xh], extra_ref.at[place], rs_send.at[1], rs_recv.at[1], device(xh, yh, ch, z))

    for step in PLANE_STEPS:
        px, py, pc = plane_peer(step)
        send(part_ref.at[pc * TILES + NY * px + py], main_ref.at[place], rs_send.at[0], rs_recv.at[0], device(px, py, pc, z))

    main_ref[place] = part_ref[own]
    extra_ref[place] = part_ref[spare]
    arrived(main_ref.at[pl.ds(0, OTHERS)], rs_recv.at[0])
    deep_ref[0, z] = jnp.sum(main_ref[...].astype(F32), axis=0).astype(BF16)

    def drain_scatter():
        arrived(part_ref.at[pl.ds(0, OTHERS)], rs_send.at[0])

        @pl.when(holder)
        def _():
            arrived(part_ref.at[pl.ds(0, len(HOLDERS) - 1)], rs_send.at[1])

        @pl.when(jnp.logical_not(holder))
        def _():
            arrived(part_ref.at[pl.ds(0, len(HOLDERS))], rs_send.at[1])

    deep_device = [device(x, y, c, ahead(z, step, NZ)) for step in DEPTH_STEPS]
    for where in deep_device[:FAR]:
        send(deep_ref.at[0, z], deep_ref.at[0, z], d_send.at[0], d_recv.at[0], where)

    @pl.when(holder)
    def _():
        arrived(extra_ref.at[pl.ds(0, OTHERS)], rs_recv.at[1])
        deep_ref[1, z] = jnp.sum(extra_ref[...].astype(F32), axis=0).astype(BF16)
        for where in deep_device[:FAR]:
            send(deep_ref.at[1, z], deep_ref.at[1, z], d_send.at[1], d_recv.at[1], where)

    for where in deep_device[FAR:]:
        send(deep_ref.at[0, z], deep_ref.at[0, z], d_send.at[0], d_recv.at[0], where)

    @pl.when(holder)
    def _():
        for where in deep_device[FAR:]:
            send(deep_ref.at[1, z], deep_ref.at[1, z], d_send.at[1], d_recv.at[1], where)

    arrived(deep_ref.at[0, pl.ds(0, DEEP)], d_recv.at[0])
    left_ref[own] = jnp.sum(deep_ref[0].astype(F32), axis=0).astype(BF16)

    def drain_depth():
        arrived(deep_ref.at[0, pl.ds(0, DEEP)], d_send.at[0])

        @pl.when(holder)
        def _():
            arrived(deep_ref.at[1, pl.ds(0, DEEP)], d_send.at[1])

    plane_device = [device(*plane_peer(step), z) for step in PLANE_STEPS]
    for where in plane_device:
        send(left_ref.at[own], left_ref.at[own], ag_send.at[0], ag_recv.at[0], where)

    @pl.when(holder)
    def _():
        arrived(deep_ref.at[1, pl.ds(0, DEEP)], d_recv.at[1])
        left_ref[spare] = jnp.sum(deep_ref[1].astype(F32), axis=0).astype(BF16)
        for where in plane_device:
            send(left_ref.at[spare], left_ref.at[spare], ag_send.at[1], ag_recv.at[1], where)

    def columns(first, last):
        return jnp.concatenate(
            [jnp.concatenate([left_ref[h * TILES + n] for h in range(NC)], axis=0) for n in range(first, last)], axis=1
        )

    arrived(left_ref.at[pl.ds(0, OTHERS)], ag_recv.at[0])

    left = columns(0, MAIN)
    product = lax.dot_general(left, l_ref[:, :MAIN * LANES], NT, preferred_element_type=F32)

    @pl.when(holder)
    def _():
        arrived(left_ref.at[pl.ds(0, len(HOLDERS) - 1)], ag_recv.at[1])

    @pl.when(jnp.logical_not(holder))
    def _():
        arrived(left_ref.at[pl.ds(0, len(HOLDERS))], ag_recv.at[1])

    rest = columns(MAIN, TILES)
    product = product + lax.dot_general(rest, l_ref[:, MAIN * LANES:], NT, preferred_element_type=F32)
    left = jnp.concatenate([left, rest], axis=1)
    t_ref[tp] = product.astype(BF16)

    def drain_gather():
        arrived(left_ref.at[pl.ds(0, OTHERS)], ag_send.at[0])

        @pl.when(holder)
        def _():
            arrived(left_ref.at[pl.ds(0, OTHERS)], ag_send.at[1])

    for step in GROUP_STEPS:
        px, py, pc = plane_peer(step)
        send(t_ref.at[tp], t_ref.at[tp], t_send, t_recv, (dp, py * NC + pc))
    right = jnp.dot(left, f_ref[...], preferred_element_type=F32)
    arrived(t_ref.at[pl.ds(0, GROUP - 1)], t_recv)
    gathered = jnp.concatenate([t_ref[t] for t in range(GROUP)], axis=1)

    keeper = x // 2 == c
    odd = NX + x % 2
    row_device = [device(ahead(x, step, NX), y, c, z) for step in ROW_STEPS]
    for j in reversed(range(FEATURES // LANES)):
        lanes = slice(j * LANES, (j + 1) * LANES)
        got = right[:, lanes] + jnp.dot(gathered, v_ref[:, lanes], preferred_element_type=F32)
        for h in range(NC):
            tile = j * NC + h
            ys_ref[tile] = got[h * HALF:(h + 1) * HALF]
            if tile < NX:

                @pl.when(x != tile)
                def _():
                    send(ys_ref.at[tile], xr_ref.at[0, x], x_send.at[0], x_recv.at[0], device(tile, y, c, z))
            else:
                taker = 2 * c + tile - NX

                @pl.when(x != taker)
                def _():
                    send(ys_ref.at[tile], xr_ref.at[1, x], x_send.at[1 + tile - NX], x_recv.at[1], device(taker, y, c, z))

    xr_ref[0, x] = ys_ref[x]
    xr_ref[1, x] = ys_ref[odd]
    arrived(xr_ref.at[0, pl.ds(0, NX - 1)], x_recv.at[0])
    deep2_ref[0, z] = jnp.sum(xr_ref[0], axis=0).astype(BF16)

    def drain_rows():
        arrived(t_ref.at[pl.ds(0, GROUP - 1)], t_send)
        arrived(ys_ref.at[pl.ds(0, NX - 1)], x_send.at[0])
        for e in range(2):

            @pl.when(x != 2 * c + e)
            def _():
                arrived(ys_ref.at[NX + e], x_send.at[1 + e])

    for where in deep_device[:FAR]:
        send(deep2_ref.at[0, z], deep2_ref.at[0, z], d2_send.at[0], d2_recv.at[0], where)

    @pl.when(keeper)
    def _():
        arrived(xr_ref.at[1, pl.ds(0, NX - 1)], x_recv.at[1])
        deep2_ref[1, z] = jnp.sum(xr_ref[1], axis=0).astype(BF16)
        for where in deep_device[:FAR]:
            send(deep2_ref.at[1, z], deep2_ref.at[1, z], d2_send.at[1], d2_recv.at[1], where)

    for where in deep_device[FAR:]:
        send(deep2_ref.at[0, z], deep2_ref.at[0, z], d2_send.at[0], d2_recv.at[0], where)

    @pl.when(keeper)
    def _():
        for where in deep_device[FAR:]:
            send(deep2_ref.at[1, z], deep2_ref.at[1, z], d2_send.at[1], d2_recv.at[1], where)

    arrived(zs_ref.at[pl.ds(0, GROUP - 1)], a_send)
    drain_scatter()
    drain_depth()
    drain_gather()

    tall = jnp.concatenate([left, jnp.zeros((LANES - RANK, WIDTH), BF16)], axis=0)
    table = lax.dot_general(left, tall, NT, preferred_element_type=F32)
    rows = lax.broadcasted_iota(jnp.int32, (RANK, LANES), 0)
    lanes = lax.broadcasted_iota(jnp.int32, (RANK, LANES), 1)
    table = jnp.where(lanes == rows + RANK, 1.0, table)
    for k in range(RANK):
        ratio = table[:, k:k + 1] / table[k:k + 1, k:k + 1]
        table = table - jnp.where(rows > k, ratio, 0.0) * table[k:k + 1, :]
    pivots = jnp.sum(jnp.where(lanes == rows, table, 0.0), axis=1, keepdims=True)
    inverse = jnp.where(lanes >= RANK, table, 0.0) * lax.rsqrt(pivots)

    inverse = split(inverse)

    def padded(value):
        above, below = jnp.zeros((RANK, FEATURES), BF16), jnp.zeros((LANES - 2 * RANK, FEATURES), BF16)
        return jnp.concatenate([above, value, below], axis=0)

    def solve(value):
        pieces = [value] if value.dtype == BF16 else [value.astype(BF16)]
        if value.dtype == F32:
            pieces.append((value - pieces[0].astype(F32)).astype(BF16))
        terms = [jnp.dot(inverse, padded(piece), preferred_element_type=F32) for piece in pieces]
        return sum(term[:RANK] + term[RANK:] for term in reversed(terms))

    first = (5 * tp) // 2
    window = jnp.concatenate(
        [
            jnp.concatenate([left_ref[h * TILES + first + i] for h in range(NC)], axis=0)
            for i in range(FEATURES // LANES)
        ],
        axis=1,
    )
    own_basis = solve(window) * math.sqrt(WIDTH)
    shifted = jnp.concatenate([own_basis[:, LANES // 2:], own_basis[:, :LANES // 2]], axis=1)
    share = WIDTH // GROUP
    basis_ref[...] = jnp.where(tp % 2 == 1, shifted, own_basis)[:, :share]

    def drain_depth2():
        arrived(deep2_ref.at[0, pl.ds(0, DEEP)], d2_send.at[0])

        @pl.when(keeper)
        def _():
            arrived(deep2_ref.at[1, pl.ds(0, DEEP)], d2_send.at[1])

    arrived(deep2_ref.at[0, pl.ds(0, DEEP)], d2_recv.at[0])
    yf_ref[x] = jnp.sum(deep2_ref[0].astype(F32), axis=0)
    for where in row_device:
        send(yf_ref.at[x], yf_ref.at[x], xg_send.at[0], xg_recv.at[0], where)

    @pl.when(keeper)
    def _():
        arrived(deep2_ref.at[1, pl.ds(0, DEEP)], d2_recv.at[1])
        yf_ref[odd] = jnp.sum(deep2_ref[1].astype(F32), axis=0)
        for where in row_device:
            send(yf_ref.at[odd], yf_ref.at[odd], xg_send.at[1], xg_recv.at[1 + x % 2], where)

    arrived(yf_ref.at[pl.ds(0, NX - 1)], xg_recv.at[0])
    for e in range(2):

        @pl.when(x != 2 * c + e)
        def _():
            arrived(yf_ref.at[NX + e], xg_recv.at[1 + e])

    summed = jnp.concatenate(
        [
            jnp.concatenate([yf_ref[j * NC + h] for h in range(NC)], axis=0)
            for j in range(FEATURES // LANES)
        ],
        axis=1,
    )
    next_ref[...] = solve(summed) * (1.0 / (NX * NZ))
    drain_rows()
    drain_depth2()
    arrived(yf_ref.at[pl.ds(0, NX - 1)], xg_send.at[0])

    @pl.when(keeper)
    def _():
        arrived(yf_ref.at[pl.ds(0, NX - 1)], xg_send.at[1])


def place_results(basis_ref, factor_ref, basis_out, factor_out):
    basis_out[...] = basis_ref[...]
    factor_out[...] = factor_ref[...]


def on_device(
    layer_input, queries, key_vectors, out_grad, feedback, factor_prev, token_count, segment_ids
):
    vmem = pl.BlockSpec(memory_space=pltpu.VMEM)
    anywhere = pl.BlockSpec(memory_space=pltpu.HBM)
    dma = pltpu.SemaphoreType.DMA
    basis, factor = pl.pallas_call(
        kernel,
        out_shape=(
            jax.ShapeDtypeStruct((RANK, WIDTH // GROUP), F32),
            jax.ShapeDtypeStruct((RANK, FEATURES), F32),
        ),
        in_specs=[anywhere] * 6 + [pl.BlockSpec(memory_space=pltpu.SMEM), anywhere],
        out_specs=(vmem, vmem),
        scratch_shapes=[
            pltpu.VMEM((RANK, FEATURES), F32),
            pltpu.VMEM((SLOTS // LANES, LANES), jnp.int32),
            pltpu.VMEM((SLOTS, LANES), BF16),
            pltpu.VMEM((SLOTS, LANES), BF16),
            pltpu.VMEM((SLOTS, FEATURES), BF16),
            pltpu.VMEM((SLOTS, FEATURES), BF16),
            pltpu.VMEM((SLOTS, FEATURES), BF16),
            pltpu.VMEM((WIDTH, FEATURES), BF16),
            pltpu.VMEM((LANES, WIDTH), BF16),
            pltpu.VMEM((SLOTS, FEATURES), BF16),
            pltpu.VMEM((HEADS, SLOTS, SLOTS), BF16),
            pltpu.VMEM((RANK, WIDTH), F32),
            pltpu.VMEM((GROUP, RANK, LANES), F32),
            pltpu.VMEM((GROUP, RANK, LANES), F32),
            pltpu.VMEM((NC * TILES, HALF, LANES), BF16),
            pltpu.VMEM((PLANE, HALF, LANES), BF16),
            pltpu.VMEM((PLANE, HALF, LANES), BF16),
            pltpu.VMEM((2, NZ, HALF, LANES), BF16),
            pltpu.VMEM((NC * TILES, HALF, LANES), BF16),
            pltpu.VMEM((GROUP, RANK, LANES), BF16),
            pltpu.VMEM((6, HALF, LANES), F32),
            pltpu.VMEM((2, NX, HALF, LANES), F32),
            pltpu.VMEM((2, NZ, HALF, LANES), BF16),
            pltpu.VMEM((6, HALF, LANES), F32),
            dma((HEADS + 4,)),
            dma, dma,
            dma((2,)), dma((2,)),
            dma((2,)), dma((2,)),
            dma((2,)), dma((2,)),
            dma, dma,
            dma((3,)), dma((2,)),
            dma((2,)), dma((2,)),
            dma((2,)), dma((3,)),
        ],
        compiler_params=pltpu.CompilerParams(
            collective_id=0, has_side_effects=True, vmem_limit_bytes=32 * 1024 * 1024
        ),
    )(
        *(
            pltpu.with_memory_space_constraint(value, pltpu.HBM)
            for value in (layer_input, queries, key_vectors, out_grad, feedback, factor_prev)
        ),
        token_count,
        pltpu.with_memory_space_constraint(segment_ids.reshape(SLOTS // LANES, LANES), pltpu.HBM),
    )
    return pl.pallas_call(
        place_results,
        out_shape=(
            jax.ShapeDtypeStruct((RANK, WIDTH // GROUP), F32),
            jax.ShapeDtypeStruct((RANK, FEATURES), F32),
        ),
        in_specs=[vmem, vmem],
        out_specs=(vmem, vmem),
        compiler_params=pltpu.CompilerParams(vmem_limit_bytes=4 * 1024 * 1024),
    )(basis, factor)


def solution(mesh):
    return jax.shard_map(
        on_device,
        mesh=mesh,
        in_specs=(
            P(("dp", "tp"), None),
            P("dp", "tp"),
            P("dp", "tp"),
            P("dp", "tp"),
            P("dp", "tp"),
            P(None, "tp"),
            P("dp"),
            P("dp"),
        ),
        out_specs=(P(None, "tp"), P(None, "tp")),
        check_vma=False,
    )
```

```python
import math

import jax
import jax.numpy as jnp
from jax import lax
from jax.experimental import pallas as pl
from jax.experimental.pallas import tpu as pltpu
from jax.sharding import PartitionSpec as P

MESH = pl.DeviceIdType.MESH
F32, BF16 = jnp.float32, jnp.bfloat16
NT = (((1,), (1,)), ((), ()))

NX, NY, NZ, NC = 4, 4, 16, 2
GROUP = NY * NC
PLANE = NX * GROUP
OTHERS = PLANE - 1
DEEP = NZ - 1
FAR = 7

HEAD_DIM = 128
HEADS = 3
SLOTS = 1024
WIDTH = 2560
RANK = 32
LANES = 128
HALF = 16
FEATURES = HEADS * HEAD_DIM
TILES = WIDTH // LANES
MAIN = NX * NY
BLOCK = 256
BLOCKS = SLOTS // BLOCK
MASKED = -1e30
PENALTY = 65536.0


def ahead(position, step, size):
    moved = position + step
    return jnp.where(moved >= size, moved - size, moved) if step else position


def hops(step, size):
    return min(step, size - step)


PLANE_STEPS = sorted(
    [
        (dx, dy, dc)
        for dx in range(NX)
        for dy in range(NY)
        for dc in range(NC)
        if (dx, dy, dc) != (0, 0, 0)
    ],
    key=lambda s: -(hops(s[0], NX) * 2 + hops(s[1], NY) * 2 + s[2]),
)
GROUP_STEPS = [s for s in PLANE_STEPS if s[0] == 0]
ROW_STEPS = sorted(range(1, NX), key=lambda s: -hops(s, NX))
DEPTH_STEPS = sorted(range(1, NZ), key=lambda s: -hops(s, NZ))
HOLDERS = [(xh, (xh + 2 * ch) % NY, ch) for ch in range(NC) for xh in range(NX)]


def split(value):
    high = value.astype(BF16)
    low = (value - high.astype(F32)).astype(BF16)
    return jnp.concatenate([high, low], axis=0)


def document_columns(seg, key_ref, query_ref):
    for b in range(SLOTS // LANES):
        ids = lax.broadcasted_iota(jnp.int32, (LANES, LANES), 0)
        own = jnp.where(seg[b:b + 1, :] == ids, 1.0, 0.0).T
        key_ref[b * LANES:(b + 1) * LANES, :] = own.astype(BF16)
        query_ref[b * LANES:(b + 1) * LANES, :] = ((own - 1.0) * PENALTY).astype(BF16)


def scores(head, b, k_ref, q_ref, dk_ref, dq_ref):
    lanes = slice(head * HEAD_DIM, (head + 1) * HEAD_DIM)
    low, high = b * BLOCK, (b + 1) * BLOCK
    q = jnp.concatenate([q_ref[low:high, lanes], dq_ref[low:high, :]], axis=1)
    k = jnp.concatenate([k_ref[low:high, lanes], dk_ref[low:high, :]], axis=1)
    near = lax.dot_general(k, q, NT, preferred_element_type=F32)
    key = lax.broadcasted_iota(jnp.int32, (BLOCK, BLOCK), 0)
    query = lax.broadcasted_iota(jnp.int32, (BLOCK, BLOCK), 1)
    near = jnp.where(key <= query, near, MASKED)
    top = jnp.max(near, axis=0, keepdims=True)
    parts = [near]
    if b:
        k = jnp.concatenate([k_ref[0:low, lanes], dk_ref[0:low, :]], axis=1)
        far = lax.dot_general(k, q, NT, preferred_element_type=F32)
        top = jnp.maximum(top, jnp.max(far, axis=0, keepdims=True))
        parts.append(far)
    return parts, top


def weigh(b, count, parts, top, w_ref):
    rate = HEAD_DIM ** (-0.5) * math.log2(math.e)
    low, high = b * BLOCK, (b + 1) * BLOCK
    parts = [jnp.exp2((part - top) * rate) for part in parts]
    total = sum(jnp.sum(part, axis=0, keepdims=True) for part in parts)
    live = lax.broadcasted_iota(jnp.int32, (1, BLOCK), 1) + low < count
    scale = jnp.where(live, 1.0 / jnp.maximum(total, 1.0), 0.0)
    for part, (start, end) in zip(parts, ((low, high), (0, low))):
        w_ref[start:end, low:high] = (part * scale).astype(BF16)


def combine(head, b, g_ref, w_ref, v_ref):
    lanes = slice(head * HEAD_DIM, (head + 1) * HEAD_DIM)
    low, high = b * BLOCK, (b + 1) * BLOCK
    v = jnp.dot(w_ref[low:high, low:], g_ref[low:, lanes], preferred_element_type=F32)
    v_ref[low:high, lanes] = v.astype(BF16)


def kernel(
    layer_hbm, q_hbm, k_hbm, g_hbm, feedback_hbm, factor_hbm, count_ref, segment_hbm,
    basis_ref, next_ref,
    factor_ref, segment_ref, dk_ref, dq_ref,
    q_ref, k_ref, g_ref, f_ref, l_ref, v_ref, w_ref, pf_ref,
    zs_ref, zr_ref, part_ref, main_ref, extra_ref, deep_ref, left_ref, t_ref, ys_ref, xr_ref, deep2_ref, yf_ref,
    load_sem,
    a_send, a_recv, rs_send, rs_recv, d_send, d_recv, ag_send, ag_recv,
    t_send, t_recv, x_send, x_recv, d2_send, d2_recv, xg_send, xg_recv,
):
    dp, tp = lax.axis_index("dp"), lax.axis_index("tp")
    x, z = dp // NZ, dp % NZ
    y, c = tp // NC, tp % NC
    place = x * GROUP + tp

    def plane_peer(step):
        dx, dy, dc = step
        return ahead(x, dx, NX), ahead(y, dy, NY), 1 - c if dc else c

    def device(px, py, pc, pz):
        return (px * NZ + pz, py * NC + pc)

    def load(source, target, which):
        pltpu.make_async_copy(source, target, load_sem.at[which]).start()

    def load_head(head):
        lanes = pl.ds(head * HEAD_DIM, HEAD_DIM)
        for source, target in ((k_hbm, k_ref), (q_hbm, q_ref), (g_hbm, g_ref)):
            load(source.at[:, lanes], target.at[:, lanes], head)

    barrier = pltpu.get_barrier_semaphore()
    for step in DEPTH_STEPS:
        pl.semaphore_signal(barrier, inc=1, device_id=device(x, y, c, ahead(z, step, NZ)), device_id_type=MESH)
    load(segment_hbm, segment_ref, HEADS)
    load_head(0)
    for step in PLANE_STEPS:
        pl.semaphore_signal(barrier, inc=1, device_id=device(*plane_peer(step), z), device_id_type=MESH)
    for head in range(1, HEADS):
        load_head(head)
    load(factor_hbm, factor_ref, HEADS + 1)
    load(feedback_hbm, f_ref, HEADS + 2)
    load(layer_hbm, l_ref, HEADS + 3)

    def send(source, target, send_sem, recv_sem, where):
        pltpu.make_async_remote_copy(
            src_ref=source, dst_ref=target, send_sem=send_sem, recv_sem=recv_sem,
            device_id=where, device_id_type=MESH,
        ).start()

    def arrived(target, recv_sem):
        pltpu.make_async_copy(target, target, recv_sem).wait()

    arrived(segment_ref, load_sem.at[HEADS])
    document_columns(segment_ref[...], dk_ref, dq_ref)
    per = BLOCK // LANES
    units = [(head, b) for b in reversed(range(BLOCKS)) for head in range(HEADS)]

    def begin(unit):
        head, b = units[unit]
        if b == BLOCKS - 1:
            arrived(k_ref, load_sem.at[head])
        return scores(head, b, k_ref, q_ref, dk_ref, dq_ref)

    ready = [begin(unit) for unit in range(1)]
    waiting = []
    for unit, (head, b) in enumerate(units):
        if unit + 1 < len(units):
            ready.append(begin(unit + 1))
        weigh(b, count_ref[0], *ready.pop(0), w_ref.at[head])
        waiting.append((head, b))
        if len(waiting) > 1:
            last, block = waiting.pop(0)
            combine(last, block, g_ref, w_ref.at[last], v_ref)
    for last, block in waiting:
        combine(last, block, g_ref, w_ref.at[last], v_ref)

    arrived(factor_ref, load_sem.at[HEADS + 1])
    factor = split(factor_ref[...])
    for t in range(GROUP):
        got = lax.dot_general(factor, v_ref[t * LANES:(t + 1) * LANES, :], NT, preferred_element_type=F32)
        zs_ref[t] = (got[:RANK] + got[RANK:]).astype(BF16)
    pl.semaphore_wait(barrier, len(DEPTH_STEPS) + len(PLANE_STEPS))
    for step in GROUP_STEPS:
        px, py, pc = plane_peer(step)
        peer = py * NC + pc
        send(zs_ref.at[peer], zr_ref.at[tp], a_send, a_recv, (dp, peer))
    zr_ref[tp] = zs_ref[tp]

    arrived(f_ref, load_sem.at[HEADS + 2])
    for j in range(WIDTH // BLOCK):
        got = lax.dot_general(factor, f_ref[j * BLOCK:(j + 1) * BLOCK, :], NT, preferred_element_type=F32)
        pf_ref[:, j * BLOCK:(j + 1) * BLOCK] = got[:RANK] + got[RANK:]
    arrived(l_ref, load_sem.at[HEADS + 3])
    arrived(zr_ref.at[pl.ds(0, GROUP - 1)], a_recv)
    mixed = split(jnp.sum(zr_ref[...].astype(F32), axis=0))
    for j in range(WIDTH // BLOCK):
        lanes = slice(j * BLOCK, (j + 1) * BLOCK)
        got = jnp.dot(mixed, l_ref[:, lanes], preferred_element_type=F32)
        part = (pf_ref[:, lanes] + got[:RANK] + got[RANK:]).astype(BF16)
        for i in range(per):
            for h in range(NC):
                part_ref[h * TILES + j * per + i] = part[h * HALF:(h + 1) * HALF, i * LANES:(i + 1) * LANES]

    holder = y == (x + 2 * c) % NY
    own = c * TILES + NY * x + y
    spare = c * TILES + MAIN + x
    for xh, yh, ch in HOLDERS:

        @pl.when(place != xh * GROUP + yh * NC + ch)
        def _():
            send(part_ref.at[ch * TILES + MAIN + xh], extra_ref.at[place], rs_send.at[1], rs_recv.at[1], device(xh, yh, ch, z))

    for step in PLANE_STEPS:
        px, py, pc = plane_peer(step)
        send(part_ref.at[pc * TILES + NY * px + py], main_ref.at[place], rs_send.at[0], rs_recv.at[0], device(px, py, pc, z))

    main_ref[place] = part_ref[own]
    extra_ref[place] = part_ref[spare]
    arrived(main_ref.at[pl.ds(0, OTHERS)], rs_recv.at[0])
    deep_ref[0, z] = jnp.sum(main_ref[...].astype(F32), axis=0).astype(BF16)

    def drain_scatter():
        arrived(part_ref.at[pl.ds(0, OTHERS)], rs_send.at[0])

        @pl.when(holder)
        def _():
            arrived(part_ref.at[pl.ds(0, len(HOLDERS) - 1)], rs_send.at[1])

        @pl.when(jnp.logical_not(holder))
        def _():
            arrived(part_ref.at[pl.ds(0, len(HOLDERS))], rs_send.at[1])

    deep_device = [device(x, y, c, ahead(z, step, NZ)) for step in DEPTH_STEPS]
    for where in deep_device[:FAR]:
        send(deep_ref.at[0, z], deep_ref.at[0, z], d_send.at[0], d_recv.at[0], where)

    @pl.when(holder)
    def _():
        arrived(extra_ref.at[pl.ds(0, OTHERS)], rs_recv.at[1])
        deep_ref[1, z] = jnp.sum(extra_ref[...].astype(F32), axis=0).astype(BF16)
        for where in deep_device[:FAR]:
            send(deep_ref.at[1, z], deep_ref.at[1, z], d_send.at[1], d_recv.at[1], where)

    for where in deep_device[FAR:]:
        send(deep_ref.at[0, z], deep_ref.at[0, z], d_send.at[0], d_recv.at[0], where)

    @pl.when(holder)
    def _():
        for where in deep_device[FAR:]:
            send(deep_ref.at[1, z], deep_ref.at[1, z], d_send.at[1], d_recv.at[1], where)

    arrived(deep_ref.at[0, pl.ds(0, DEEP)], d_recv.at[0])
    left_ref[own] = jnp.sum(deep_ref[0].astype(F32), axis=0).astype(BF16)

    def drain_depth():
        arrived(deep_ref.at[0, pl.ds(0, DEEP)], d_send.at[0])

        @pl.when(holder)
        def _():
            arrived(deep_ref.at[1, pl.ds(0, DEEP)], d_send.at[1])

    plane_device = [device(*plane_peer(step), z) for step in PLANE_STEPS]
    for where in plane_device:
        send(left_ref.at[own], left_ref.at[own], ag_send.at[0], ag_recv.at[0], where)

    @pl.when(holder)
    def _():
        arrived(deep_ref.at[1, pl.ds(0, DEEP)], d_recv.at[1])
        left_ref[spare] = jnp.sum(deep_ref[1].astype(F32), axis=0).astype(BF16)
        for where in plane_device:
            send(left_ref.at[spare], left_ref.at[spare], ag_send.at[1], ag_recv.at[1], where)

    def columns(first, last):
        return jnp.concatenate(
            [jnp.concatenate([left_ref[h * TILES + n] for h in range(NC)], axis=0) for n in range(first, last)], axis=1
        )

    arrived(left_ref.at[pl.ds(0, OTHERS)], ag_recv.at[0])

    left = columns(0, MAIN)
    product = lax.dot_general(left, l_ref[:, :MAIN * LANES], NT, preferred_element_type=F32)

    @pl.when(holder)
    def _():
        arrived(left_ref.at[pl.ds(0, len(HOLDERS) - 1)], ag_recv.at[1])

    @pl.when(jnp.logical_not(holder))
    def _():
        arrived(left_ref.at[pl.ds(0, len(HOLDERS))], ag_recv.at[1])

    rest = columns(MAIN, TILES)
    product = product + lax.dot_general(rest, l_ref[:, MAIN * LANES:], NT, preferred_element_type=F32)
    left = jnp.concatenate([left, rest], axis=1)
    t_ref[tp] = product.astype(BF16)

    def drain_gather():
        arrived(left_ref.at[pl.ds(0, OTHERS)], ag_send.at[0])

        @pl.when(holder)
        def _():
            arrived(left_ref.at[pl.ds(0, OTHERS)], ag_send.at[1])

    for step in GROUP_STEPS:
        px, py, pc = plane_peer(step)
        send(t_ref.at[tp], t_ref.at[tp], t_send, t_recv, (dp, py * NC + pc))
    right = jnp.dot(left, f_ref[...], preferred_element_type=F32)
    arrived(t_ref.at[pl.ds(0, GROUP - 1)], t_recv)
    gathered = jnp.concatenate([t_ref[t] for t in range(GROUP)], axis=1)

    keeper = x // 2 == c
    odd = NX + x % 2
    row_device = [device(ahead(x, step, NX), y, c, z) for step in ROW_STEPS]
    for j in reversed(range(FEATURES // LANES)):
        lanes = slice(j * LANES, (j + 1) * LANES)
        got = right[:, lanes] + jnp.dot(gathered, v_ref[:, lanes], preferred_element_type=F32)
        for h in range(NC):
            tile = j * NC + h
            ys_ref[tile] = got[h * HALF:(h + 1) * HALF]
            if tile < NX:

                @pl.when(x != tile)
                def _():
                    send(ys_ref.at[tile], xr_ref.at[0, x], x_send.at[0], x_recv.at[0], device(tile, y, c, z))
            else:
                taker = 2 * c + tile - NX

                @pl.when(x != taker)
                def _():
                    send(ys_ref.at[tile], xr_ref.at[1, x], x_send.at[1 + tile - NX], x_recv.at[1], device(taker, y, c, z))

    xr_ref[0, x] = ys_ref[x]
    xr_ref[1, x] = ys_ref[odd]
    arrived(xr_ref.at[0, pl.ds(0, NX - 1)], x_recv.at[0])
    deep2_ref[0, z] = jnp.sum(xr_ref[0], axis=0).astype(BF16)

    def drain_rows():
        arrived(t_ref.at[pl.ds(0, GROUP - 1)], t_send)
        arrived(ys_ref.at[pl.ds(0, NX - 1)], x_send.at[0])
        for e in range(2):

            @pl.when(x != 2 * c + e)
            def _():
                arrived(ys_ref.at[NX + e], x_send.at[1 + e])

    for where in deep_device[:FAR]:
        send(deep2_ref.at[0, z], deep2_ref.at[0, z], d2_send.at[0], d2_recv.at[0], where)

    @pl.when(keeper)
    def _():
        arrived(xr_ref.at[1, pl.ds(0, NX - 1)], x_recv.at[1])
        deep2_ref[1, z] = jnp.sum(xr_ref[1], axis=0).astype(BF16)
        for where in deep_device[:FAR]:
            send(deep2_ref.at[1, z], deep2_ref.at[1, z], d2_send.at[1], d2_recv.at[1], where)

    for where in deep_device[FAR:]:
        send(deep2_ref.at[0, z], deep2_ref.at[0, z], d2_send.at[0], d2_recv.at[0], where)

    @pl.when(keeper)
    def _():
        for where in deep_device[FAR:]:
            send(deep2_ref.at[1, z], deep2_ref.at[1, z], d2_send.at[1], d2_recv.at[1], where)

    arrived(zs_ref.at[pl.ds(0, GROUP - 1)], a_send)
    drain_scatter()
    drain_depth()
    drain_gather()

    tall = jnp.concatenate([left, jnp.zeros((LANES - RANK, WIDTH), BF16)], axis=0)
    table = lax.dot_general(left, tall, NT, preferred_element_type=F32)
    rows = lax.broadcasted_iota(jnp.int32, (RANK, LANES), 0)
    lanes = lax.broadcasted_iota(jnp.int32, (RANK, LANES), 1)
    table = jnp.where(lanes == rows + RANK, 1.0, table)
    for k in range(RANK):
        ratio = table[:, k:k + 1] / table[k:k + 1, k:k + 1]
        table = table - jnp.where(rows > k, ratio, 0.0) * table[k:k + 1, :]
    pivots = jnp.sum(jnp.where(lanes == rows, table, 0.0), axis=1, keepdims=True)
    inverse = jnp.where(lanes >= RANK, table, 0.0) * lax.rsqrt(pivots)

    inverse = split(inverse)

    def padded(value):
        above, below = jnp.zeros((RANK, FEATURES), BF16), jnp.zeros((LANES - 2 * RANK, FEATURES), BF16)
        return jnp.concatenate([above, value, below], axis=0)

    def solve(value):
        pieces = [value] if value.dtype == BF16 else [value.astype(BF16)]
        if value.dtype == F32:
            pieces.append((value - pieces[0].astype(F32)).astype(BF16))
        terms = [jnp.dot(inverse, padded(piece), preferred_element_type=F32) for piece in pieces]
        return sum(term[:RANK] + term[RANK:] for term in reversed(terms))

    first = (5 * tp) // 2
    window = jnp.concatenate(
        [
            jnp.concatenate([left_ref[h * TILES + first + i] for h in range(NC)], axis=0)
            for i in range(FEATURES // LANES)
        ],
        axis=1,
    )
    own_basis = solve(window) * math.sqrt(WIDTH)
    shifted = jnp.concatenate([own_basis[:, LANES // 2:], own_basis[:, :LANES // 2]], axis=1)
    share = WIDTH // GROUP
    basis_ref[...] = jnp.where(tp % 2 == 1, shifted, own_basis)[:, :share]

    def drain_depth2():
        arrived(deep2_ref.at[0, pl.ds(0, DEEP)], d2_send.at[0])

        @pl.when(keeper)
        def _():
            arrived(deep2_ref.at[1, pl.ds(0, DEEP)], d2_send.at[1])

    arrived(deep2_ref.at[0, pl.ds(0, DEEP)], d2_recv.at[0])
    yf_ref[x] = jnp.sum(deep2_ref[0].astype(F32), axis=0)
    for where in row_device:
        send(yf_ref.at[x], yf_ref.at[x], xg_send.at[0], xg_recv.at[0], where)

    @pl.when(keeper)
    def _():
        arrived(deep2_ref.at[1, pl.ds(0, DEEP)], d2_recv.at[1])
        yf_ref[odd] = jnp.sum(deep2_ref[1].astype(F32), axis=0)
        for where in row_device:
            send(yf_ref.at[odd], yf_ref.at[odd], xg_send.at[1], xg_recv.at[1 + x % 2], where)

    arrived(yf_ref.at[pl.ds(0, NX - 1)], xg_recv.at[0])
    for e in range(2):

        @pl.when(x != 2 * c + e)
        def _():
            arrived(yf_ref.at[NX + e], xg_recv.at[1 + e])

    summed = jnp.concatenate(
        [
            jnp.concatenate([yf_ref[j * NC + h] for h in range(NC)], axis=0)
            for j in range(FEATURES // LANES)
        ],
        axis=1,
    )
    next_ref[...] = solve(summed) * (1.0 / (NX * NZ))
    drain_rows()
    drain_depth2()
    arrived(yf_ref.at[pl.ds(0, NX - 1)], xg_send.at[0])

    @pl.when(keeper)
    def _():
        arrived(yf_ref.at[pl.ds(0, NX - 1)], xg_send.at[1])


def place_results(basis_ref, factor_ref, basis_out, factor_out):
    basis_out[...] = basis_ref[...]
    factor_out[...] = factor_ref[...]


def on_device(
    layer_input, queries, key_vectors, out_grad, feedback, factor_prev, token_count, segment_ids
):
    vmem = pl.BlockSpec(memory_space=pltpu.VMEM)
    anywhere = pl.BlockSpec(memory_space=pltpu.HBM)
    dma = pltpu.SemaphoreType.DMA
    basis, factor = pl.pallas_call(
        kernel,
        out_shape=(
            jax.ShapeDtypeStruct((RANK, WIDTH // GROUP), F32),
            jax.ShapeDtypeStruct((RANK, FEATURES), F32),
        ),
        in_specs=[anywhere] * 6 + [pl.BlockSpec(memory_space=pltpu.SMEM), anywhere],
        out_specs=(vmem, vmem),
        scratch_shapes=[
            pltpu.VMEM((RANK, FEATURES), F32),
            pltpu.VMEM((SLOTS // LANES, LANES), jnp.int32),
            pltpu.VMEM((SLOTS, LANES), BF16),
            pltpu.VMEM((SLOTS, LANES), BF16),
            pltpu.VMEM((SLOTS, FEATURES), BF16),
            pltpu.VMEM((SLOTS, FEATURES), BF16),
            pltpu.VMEM((SLOTS, FEATURES), BF16),
            pltpu.VMEM((WIDTH, FEATURES), BF16),
            pltpu.VMEM((LANES, WIDTH), BF16),
            pltpu.VMEM((SLOTS, FEATURES), BF16),
            pltpu.VMEM((HEADS, SLOTS, SLOTS), BF16),
            pltpu.VMEM((RANK, WIDTH), F32),
            pltpu.VMEM((GROUP, RANK, LANES), BF16),
            pltpu.VMEM((GROUP, RANK, LANES), BF16),
            pltpu.VMEM((NC * TILES, HALF, LANES), BF16),
            pltpu.VMEM((PLANE, HALF, LANES), BF16),
            pltpu.VMEM((PLANE, HALF, LANES), BF16),
            pltpu.VMEM((2, NZ, HALF, LANES), BF16),
            pltpu.VMEM((NC * TILES, HALF, LANES), BF16),
            pltpu.VMEM((GROUP, RANK, LANES), BF16),
            pltpu.VMEM((6, HALF, LANES), F32),
            pltpu.VMEM((2, NX, HALF, LANES), F32),
            pltpu.VMEM((2, NZ, HALF, LANES), BF16),
            pltpu.VMEM((6, HALF, LANES), F32),
            dma((HEADS + 4,)),
            dma, dma,
            dma((2,)), dma((2,)),
            dma((2,)), dma((2,)),
            dma((2,)), dma((2,)),
            dma, dma,
            dma((3,)), dma((2,)),
            dma((2,)), dma((2,)),
            dma((2,)), dma((3,)),
        ],
        compiler_params=pltpu.CompilerParams(
            collective_id=0, has_side_effects=True, vmem_limit_bytes=32 * 1024 * 1024
        ),
    )(
        *(
            pltpu.with_memory_space_constraint(value, pltpu.HBM)
            for value in (layer_input, queries, key_vectors, out_grad, feedback, factor_prev)
        ),
        token_count,
        pltpu.with_memory_space_constraint(segment_ids.reshape(SLOTS // LANES, LANES), pltpu.HBM),
    )
    return pl.pallas_call(
        place_results,
        out_shape=(
            jax.ShapeDtypeStruct((RANK, WIDTH // GROUP), F32),
            jax.ShapeDtypeStruct((RANK, FEATURES), F32),
        ),
        in_specs=[vmem, vmem],
        out_specs=(vmem, vmem),
        compiler_params=pltpu.CompilerParams(vmem_limit_bytes=4 * 1024 * 1024),
    )(basis, factor)


def solution(mesh):
    return jax.shard_map(
        on_device,
        mesh=mesh,
        in_specs=(
            P(("dp", "tp"), None),
            P("dp", "tp"),
            P("dp", "tp"),
            P("dp", "tp"),
            P("dp", "tp"),
            P(None, "tp"),
            P("dp"),
            P("dp"),
        ),
        out_specs=(P(None, "tp"), P(None, "tp")),
        check_vma=False,
    )
```
